256 devices in a mesh: member: 8 (over z_hi, core), grid: 32 (over y, z_lo, x).
Axes of the slice: x: 4, y: 4, z: 8 (z_hi: 4, z_lo: 2; z = z_hi * 2 + z_lo), core: 2. Of those that a mesh axis runs over, the one named last changes fastest.
Arguments:
- inputs: bfloat16 [8, 8192, 1024], P('member', 'grid'), may hold values from -6 to 6
- norm_gain: float32 [1024], replicated, may hold values from 0.25 to 1.75
- w_query: bfloat16 [1024, 1024], replicated, may hold values from -0.1875 to 0.1875
- w_key: bfloat16 [1024, 1024], replicated, may hold values from -0.1875 to 0.1875
- w_value: bfloat16 [1024, 1024], replicated, may hold values from -0.1875 to 0.1875
- w_out: bfloat16 [1024, 1024], replicated, may hold values from -0.1875 to 0.1875
- w_decode: bfloat16 [1024, 128], replicated, may hold values from -0.1875 to 0.1875
- point_node: int32 [32768], P('grid'), may hold values from 0 to 8191, as said below
- truth: float32 [128, 32768], P(None, 'grid'), may hold values from -6 to 6
Outputs:
- crps_terms: float32 [8, 128, 32768], P('member', None, 'grid')
- grad_value: float32 [1024, 1024], P('grid', 'member')
The draws below stay inside these ranges and needn't reach their ends.
Inputs may be any that keep to these rules, and one draw needn't show every extreme that they name: `point_node`: the grid points of the r-th block of 1024 read nodes of the r-th band r * 256 to (r + 1) * 256 - 1.
All inputs are finite; a program needn't handle non-finite values.
Results may differ from the reference program's by a relative error of at most 0.035.
Values may be sent and summed in bfloat16 or wider, within the bound.
No kernel may reach another device: no remote copies, remote signals or barrier semaphores. Data moves between devices by JAX's collectives and lax.ppermute only.
A program may use at most 64 MiB of HBM per device.

```python
import jax
import jax.numpy as jnp
from jax import lax

D = 1024
HEADS = 16
HD = 64
CH = 128
NODE_DEV = 256
G_DEV = 1024
HALO = 128
MEMBERS = 8
NODES = 8192
GRID_PTS = 32768


def draw_point_node(key, part):
    key = jax.random.fold_in(key, 11)
    band_count = GRID_PTS // G_DEV
    local_node = jax.random.randint(key, (band_count, G_DEV), 0, NODE_DEV, dtype=jnp.int32)
    local_node = local_node.at[:, 0].set(NODE_DEV - 1)
    local_node = local_node.at[:, 1].set(0)
    band_start = jnp.arange(band_count, dtype=jnp.int32)[:, None] * NODE_DEV
    return (local_node + band_start).reshape(-1).astype(jnp.int32)


def block_levels(stream_key, extent, pieces, smallest, largest):
    def one(position, parts):
        draws = jax.random.uniform(jax.random.fold_in(jax.random.fold_in(stream_key, 6), position), (parts,), jnp.float32, smallest / len(pieces), largest / len(pieces))
        return jnp.repeat(jnp.exp(draws), extent[position] // parts).reshape((-1,) + (1,) * (len(extent) - position - 1))

    level = one(*pieces[0])
    for cut in pieces[1:]:
        level = level * one(*cut)
    return level


def bell_draw(stream_key, extent, width, most, split=(), kind=jnp.bfloat16):
    drawn = jax.random.normal(stream_key, extent, jnp.float32) * width
    if len(split) > 0:
        drawn = block_levels(stream_key, extent, split, -0.22, 0.18) * drawn
    return jnp.clip(drawn, min=-most, max=most).astype(kind)


def setup_inputs(seed: int = 0) -> dict:
    key_list = jax.random.split(jax.random.key(seed), 10)
    return {
        "inputs": bell_draw(key_list[0], (MEMBERS, NODES, D), 1.0, 6.0, ((0, 8), (1, 32))),
        "norm_gain": jnp.clip(1.0 + 0.15 * jax.random.normal(key_list[1], (D,), jnp.float32), 0.25, 1.75),
        "w_query": bell_draw(key_list[2], (D, D), D ** -0.5, 0.1875),
        "w_key": bell_draw(key_list[3], (D, D), D ** -0.5, 0.1875),
        "w_value": bell_draw(key_list[4], (D, D), D ** -0.5, 0.1875),
        "w_out": bell_draw(key_list[5], (D, D), D ** -0.5, 0.1875),
        "w_decode": bell_draw(key_list[6], (D, CH), D ** -0.5, 0.1875),
        "point_node": draw_point_node(jax.random.fold_in(key_list[9], 71), 0),
        "truth": bell_draw(key_list[8], (CH, GRID_PTS), 1.0, 6.0, ((1, 32),), jnp.float32),
    }


def rms_normed(states, norm_gain):
    floats = states.astype(jnp.float32)
    meansq = lax.optimization_barrier(jnp.mean(floats * floats, axis=-1, keepdims=True)) + 1e-05
    return (floats * lax.rsqrt(meansq) * norm_gain).astype(jnp.bfloat16)

def smooth_abs(values):
    return jnp.sqrt(values * values + 0.25)

def smooth_slope(values):
    return values / jnp.sqrt(values * values + 0.25)

def window_weights(queries, keys, first_node):
    blocklen = queries.shape[0]
    reach = (keys.shape[0] - blocklen) // 2
    scores = jnp.einsum('qhd,khd->hqk', queries.astype(jnp.float32), keys.astype(jnp.float32)) * 0.125
    query_pos = jnp.arange(blocklen)[:, None]
    key_pos = jnp.arange(keys.shape[0])[None, :]
    global_pos = first_node + key_pos - reach
    valid = (jnp.abs(key_pos - query_pos - reach) <= reach) & (global_pos >= 0) & (global_pos < NODES)
    scores = jnp.where(valid[None], scores, -1e+30)
    row_max = lax.optimization_barrier(jnp.max(scores, axis=-1, keepdims=True))
    weights = jnp.exp(scores - row_max)
    return (weights / lax.optimization_barrier(jnp.sum(weights, axis=-1, keepdims=True))).astype(jnp.bfloat16)

def projections(states, norm_gain, w_query, w_key, w_value):
    normed = rms_normed(states, norm_gain)
    queries = jnp.dot(normed, w_query, preferred_element_type=jnp.float32).astype(jnp.bfloat16).reshape(NODES, HEADS, HD)
    keys = jnp.dot(normed, w_key, preferred_element_type=jnp.float32).astype(jnp.bfloat16).reshape(NODES, HEADS, HD)
    values = jnp.dot(normed, w_value, preferred_element_type=jnp.float32).astype(jnp.bfloat16).reshape(NODES, HEADS, HD)
    padded_keys = jnp.pad(keys, ((HALO, HALO), (0, 0), (0, 0)))
    padded_values = jnp.pad(values, ((HALO, HALO), (0, 0), (0, 0)))
    return (normed, queries, padded_keys, padded_values)

def reference(inputs, norm_gain, w_query, w_key, w_value, w_out, w_decode, point_node, truth):

    def one_member(states):
        normed, queries, padded_keys, padded_values = projections(states, norm_gain, w_query, w_key, w_value)

        def block_at(block_index):
            first = (block_index * NODE_DEV).astype(jnp.int32)
            query_rows = lax.dynamic_slice_in_dim(queries, first, NODE_DEV, 0)
            key_rows = lax.dynamic_slice_in_dim(padded_keys, first, NODE_DEV + 2 * HALO, 0)
            value_rows = lax.dynamic_slice_in_dim(padded_values, first, NODE_DEV + 2 * HALO, 0)
            weights = window_weights(query_rows, key_rows, first)
            mixed = jnp.einsum('hqk,khd->qhd', weights.astype(jnp.float32), value_rows.astype(jnp.float32))
            return mixed.reshape(NODE_DEV, D).astype(jnp.bfloat16)
        mixed = lax.map(block_at, jnp.arange(NODES // NODE_DEV, dtype=jnp.int32)).reshape(NODES, D)
        projected = jnp.dot(mixed, w_out, preferred_element_type=jnp.float32)
        hidden = (states.astype(jnp.float32) + projected).astype(jnp.bfloat16)
        return jnp.dot(hidden, w_decode, preferred_element_type=jnp.float32)
    decoded_all = lax.map(one_member, inputs)
    pred = jnp.transpose(decoded_all[:, point_node, :], (0, 2, 1))
    member_count = MEMBERS

    def pair_terms(one_pred):
        pair_diff = one_pred[None] - pred
        return (lax.optimization_barrier(jnp.sum(smooth_abs(pair_diff), axis=0)), lax.optimization_barrier(jnp.sum(smooth_slope(pair_diff), axis=0)))
    spread, slope_total = lax.map(pair_terms, pred)
    error_value = pred - truth[None]
    crps_terms = smooth_abs(error_value) - spread / (2.0 * (member_count - 1))
    loss_grad = (smooth_slope(error_value) - slope_total / (member_count - 1)) / member_count
    decode_float = w_decode.astype(jnp.float32)

    def member_grad(packed):
        states, grad_rows = packed
        normed, queries, padded_keys, padded_values = projections(states, norm_gain, w_query, w_key, w_value)
        node_grad = jax.ops.segment_sum(grad_rows.T, point_node, NODES)
        hidden_grad = jnp.dot(node_grad, decode_float.T, precision=lax.Precision.HIGHEST).astype(jnp.bfloat16)
        mixed_grad = jnp.dot(hidden_grad, w_out.T, preferred_element_type=jnp.float32).astype(jnp.bfloat16).reshape(NODES, HEADS, HD)

        def add_block(block_index, accum):
            first = (block_index * NODE_DEV).astype(jnp.int32)
            query_rows = lax.dynamic_slice_in_dim(queries, first, NODE_DEV, 0)
            key_rows = lax.dynamic_slice_in_dim(padded_keys, first, NODE_DEV + 2 * HALO, 0)
            weights = window_weights(query_rows, key_rows, first)
            grad_rows_block = lax.dynamic_slice_in_dim(mixed_grad, first, NODE_DEV, 0)
            contrib = jnp.einsum('hqk,qhd->khd', weights.astype(jnp.float32), grad_rows_block.astype(jnp.float32))
            current = lax.dynamic_slice_in_dim(accum, first, NODE_DEV + 2 * HALO, 0)
            return lax.dynamic_update_slice_in_dim(accum, current + contrib, first, 0)
        start_accum = jnp.zeros((NODES + 2 * HALO, HEADS, HD), jnp.float32)
        accum = lax.fori_loop(0, NODES // NODE_DEV, add_block, start_accum)
        value_grad = accum[HALO:HALO + NODES].reshape(NODES, D).astype(jnp.bfloat16)
        return jnp.dot(normed.T, value_grad, preferred_element_type=jnp.float32)
    grads = lax.map(member_grad, (inputs, loss_grad))
    grad_value = lax.optimization_barrier(jnp.sum(grads, axis=0))
    return (crps_terms, grad_value)
```

```python
import jax
import jax.numpy as jnp
from jax import lax
from jax.experimental import pallas as pl
from jax.experimental.pallas import tpu as pltpu
from jax.sharding import Mesh, PartitionSpec as P

F32 = jnp.float32
BF16 = jnp.bfloat16
ROWS = 256
REACH = 128
D = 1024
PAIRS = 8
PTS = 1024
CH = 128
MEMBERS = 8
MASKED = -1e30
GRID = ("y", "zl", "x")

NT = (((1,), (1,)), ((), ()))


def mm(a, b):
    return jnp.dot(a, b, preferred_element_type=F32)


def mm_nt(a, b):
    return lax.dot_general(a, b, NT, preferred_element_type=F32)


def rms(states, gain):
    floats = states.astype(F32)
    meansq = jnp.mean(floats * floats, axis=-1, keepdims=True) + 1e-05
    return (floats * lax.rsqrt(meansq) * gain).astype(BF16)


def thirds(values):
    first = values.astype(BF16)
    rest = values - first.astype(F32)
    second = rest.astype(BF16)
    third = (rest - second.astype(F32)).astype(BF16)
    return first, second, third


def call(kernel, outs, cost, scratch=(), smem=0, limit=40):
    def run(*args):
        in_specs = [pl.BlockSpec(memory_space=pltpu.SMEM)] * smem
        in_specs += [pl.BlockSpec(memory_space=pltpu.VMEM)] * (len(args) - smem)
        return pl.pallas_call(
            kernel,
            out_shape=[jax.ShapeDtypeStruct(s, d) for s, d in outs],
            in_specs=in_specs,
            out_specs=[pl.BlockSpec(memory_space=pltpu.VMEM)] * len(outs),
            scratch_shapes=list(scratch),
            compiler_params=pltpu.CompilerParams(vmem_limit_bytes=limit * 2**20),
            cost_estimate=pl.CostEstimate(
                flops=int(cost * 1e9), bytes_accessed=int(cost * 3e6), transcendentals=0
            ),
        )(*args)

    return run


def project_kernel(x_ref, gain_ref, wq_ref, wk_ref, wv_ref, q_ref, k_ref, v_ref, n_ref):
    normed = rms(x_ref[...], gain_ref[...])
    n_ref[...] = normed
    q_ref[...] = mm(normed, wq_ref[...]).astype(BF16) * jnp.asarray(0.125, BF16)
    k_ref[...] = mm(normed, wk_ref[...]).astype(BF16)
    v_ref[...] = mm(normed, wv_ref[...]).astype(BF16)


def attend_kernel(
    edge_ref, xb_ref, xa_ref, gain_ref, wk_ref, wv_ref, q_ref, k_ref, v_ref, x_ref, wo_ref, wd_ref,
    p_ref, dec_ref, dech_ref, nh_ref, kh, vh, mixed,
):
    gain = gain_ref[...]
    nh_ref[:REACH] = rms(xb_ref[...], gain)
    nh_ref[REACH:] = rms(xa_ref[...], gain)
    halo = nh_ref[...]
    kh[...] = mm(halo, wk_ref[...]).astype(BF16)
    vh[...] = mm(halo, wv_ref[...]).astype(BF16)
    lane = lax.broadcasted_iota(jnp.int32, (REACH, 128), 1)
    low = (lane < 64).astype(F32).astype(BF16)
    high = (lane >= 64).astype(F32).astype(BF16)
    lane_low = lane < 64
    query_o = lax.broadcasted_iota(jnp.int32, (2 * REACH, ROWS), 0) % REACH
    key_o = lax.broadcasted_iota(jnp.int32, (2 * REACH, ROWS), 1)
    query_h = lax.broadcasted_iota(jnp.int32, (2 * REACH, REACH), 0) % REACH
    key_h = lax.broadcasted_iota(jnp.int32, (2 * REACH, REACH), 1)
    for block in range(2):
        if block == 0:
            bias_o = jnp.where(key_o <= query_o + REACH, 0.0, MASKED)
            bias_h = jnp.where((key_h >= query_h) & (edge_ref[0] == 0), 0.0, MASKED)
        else:
            bias_o = jnp.where(key_o >= query_o, 0.0, MASKED)
            bias_h = jnp.where((key_h <= query_h) & (edge_ref[1] == 0), 0.0, MASKED)
        rows = slice(block * REACH, (block + 1) * REACH)
        for pair in range(PAIRS):
            cols = slice(pair * 128, (pair + 1) * 128)
            both = q_ref[rows, cols]
            stacked = jnp.concatenate([both * low, both * high], axis=0)
            so = mm_nt(stacked, k_ref[:, cols]) + bias_o
            sh = mm_nt(stacked, kh[rows, cols]) + bias_h
            top = jnp.maximum(
                jnp.max(so, axis=-1, keepdims=True), jnp.max(sh, axis=-1, keepdims=True)
            )
            eo = jnp.exp(so - top)
            eh = jnp.exp(sh - top)
            inv = 1.0 / (
                jnp.sum(eo, axis=-1, keepdims=True) + jnp.sum(eh, axis=-1, keepdims=True)
            )
            po = (eo * inv).astype(BF16)
            ph = (eh * inv).astype(BF16)
            p_ref[pair, block, :, :ROWS] = po
            p_ref[pair, block, :, ROWS:] = ph
            out = mm(po, v_ref[:, cols]) + mm(ph, vh[rows, cols])
            mixed[rows, cols] = jnp.where(lane_low, out[:REACH], out[REACH:]).astype(BF16)
    projected = mm(mixed[...], wo_ref[...])
    hidden = (x_ref[...].astype(F32) + projected).astype(BF16)
    decoded = mm(hidden, wd_ref[...]).T
    dec_ref[...] = decoded
    dech_ref[...] = decoded.astype(BF16)


def turn_kernel(n_ref, nh_ref, t_ref):
    t_ref[:, :ROWS] = n_ref[...].astype(F32).T.astype(BF16)
    t_ref[:, ROWS:] = nh_ref[...].astype(F32).T.astype(BF16)


def selector(node_ref):
    node = lax.broadcasted_iota(jnp.int32, (ROWS, PTS), 0)
    return (node == node_ref[...]).astype(F32).astype(BF16)


def truth_kernel(dec_ref, node_ref, truth_ref, abs_ref, slope_ref, count_ref):
    select = selector(node_ref)
    parts = thirds(dec_ref[...])
    pred = mm(parts[2], select) + mm(parts[1], select) + mm(parts[0], select)
    error = pred - truth_ref[...]
    square = error * error + 0.25
    inverse = lax.rsqrt(square)
    abs_ref[...] = square * inverse
    slope = error * inverse
    high = slope.astype(BF16)
    rest = (slope - high.astype(F32)).astype(BF16)
    slope_ref[...] = mm_nt(high, select) + mm_nt(rest, select)
    count_ref[...] = mm_nt(jnp.ones((16, PTS), BF16), select)[:8]


def backward_kernel(
    core_ref, dec_ref, o1_ref, oz_ref, oc_ref, slope_ref, count_ref, wd_ref, wo_ref, p_ref,
    keep_ref, send_ref, spread_ref, mg,
):
    own = dec_ref[...]
    spread = jnp.full((CH, ROWS), 0.5, F32)
    total = jnp.zeros((CH, ROWS), F32)
    others = [o1_ref[...]] + [oz_ref[i] for i in range(3)] + [oc_ref[i] for i in range(3)]
    for other in others:
        differ = own - other.astype(F32)
        square = differ * differ + 0.25
        inverse = lax.rsqrt(square)
        spread += square * inverse
        total += differ * inverse
    spread_ref[...] = spread
    node_grad = (slope_ref[...] - count_ref[:1] * total * (1.0 / (MEMBERS - 1))) * (1.0 / MEMBERS)
    high = node_grad.astype(BF16)
    rest = (node_grad - high.astype(F32)).astype(BF16)
    hidden_grad = (mm(wd_ref[...], high) + mm(wd_ref[...], rest)).astype(BF16)
    mg[...] = mm(wo_ref[...], hidden_grad).astype(BF16)
    feature = lax.broadcasted_iota(jnp.int32, (128, REACH), 0)
    low = (feature < 64).astype(F32).astype(BF16)
    high_rows = (feature >= 64).astype(F32).astype(BF16)
    core = core_ref[0]
    for which, out_ref in ((1, send_ref), (0, keep_ref)):
        for z in range(4):
            pair = 2 * z + (core + which) % 2
            grads = mg[pl.ds(pl.multiple_of(pair * 128, 128), 128), :]
            total_own = None
            rows = slice(z * 128, (z + 1) * 128)
            for block in range(2):
                part = grads[:, block * REACH : (block + 1) * REACH]
                split = jnp.concatenate([part * low, part * high_rows], axis=1)
                term = mm(split, p_ref[pair, block, :, :ROWS])
                total_own = term if block == 0 else total_own + term
                out_ref[rows, ROWS + block * REACH : ROWS + (block + 1) * REACH] = mm(
                    split, p_ref[pair, block, :, ROWS:]
                ).astype(BF16)
            out_ref[rows, :ROWS] = total_own.astype(BF16)


def product_kernel(t_ref, u_ref, keep_ref, recv_ref, out_ref):
    out_ref[...] = (
        mm_nt(t_ref[...], keep_ref[...]) + mm_nt(u_ref[...], recv_ref[...])
    ).astype(BF16)


def crps_kernel(abs_ref, spread_ref, node_ref, out_ref):
    select = selector(node_ref)
    parts = thirds(spread_ref[...])
    spread = mm(parts[2], select) + mm(parts[1], select) + mm(parts[0], select)
    out_ref[...] = abs_ref[...] - spread * (1.0 / (2.0 * (MEMBERS - 1)))


def body(inputs, norm_gain, w_query, w_key, w_value, w_out, w_decode, point_node, truth):
    states = inputs[0]
    gain = norm_gain[None]
    band = lax.axis_index(GRID)
    bands = 32
    core = lax.axis_index("core")
    edge = jnp.stack([band == 0, band == bands - 1]).astype(jnp.int32)
    node = (point_node - band * ROWS)[None]
    up = [(i, i + 1) for i in range(bands - 1)]
    down = [(i + 1, i) for i in range(bands - 1)]
    swap = [(0, 1), (1, 0)]
    before = lax.ppermute(states[REACH:], GRID, up)
    after = lax.ppermute(states[:REACH], GRID, down)
    wide = ((ROWS, D), BF16)
    queries, keys, values, normed = call(project_kernel, [wide] * 4, 1.6)(
        states, gain, w_query, w_key, w_value
    )
    probs, decoded, decoded_half, normed_halo = call(
        attend_kernel,
        [((PAIRS, 2, 2 * REACH, ROWS + REACH), BF16), ((CH, ROWS), F32), ((CH, ROWS), BF16), wide],
        4.0,
        [pltpu.VMEM((ROWS, D), BF16)] * 3,
        smem=1,
    )(edge, before, after, gain, w_key, w_value, queries, keys, values, states, w_out, w_decode)
    other = lax.ppermute(decoded_half, "core", swap)
    along = [
        lax.ppermute(decoded_half, "zh", [(i, (i + k) % 4) for i in range(4)]) for k in (2, 1, 3)
    ]
    along = jnp.stack(along)
    across = lax.ppermute(along, "core", swap)
    (turned,) = call(turn_kernel, [((D, 2 * ROWS), BF16)], 1.0)(normed, normed_halo)
    turned_other = lax.ppermute(turned, "core", swap)
    abs_error, slope, count = call(
        truth_kernel, [((CH, PTS), F32), ((CH, ROWS), F32), ((8, ROWS), F32)], 2.0
    )(decoded, node, truth)
    keep, send, spread = call(
        backward_kernel,
        [((512, 512), BF16), ((512, 512), BF16), ((CH, ROWS), F32)],
        3.0,
        [pltpu.VMEM((D, ROWS), BF16)],
        smem=1,
    )(core[None], decoded, other, along, across, slope, count, w_decode, w_out, probs)
    received = lax.ppermute(send, "core", swap)
    (crps_terms,) = call(crps_kernel, [((CH, PTS), F32)], 1.0)(abs_error, spread, node)
    (product,) = call(product_kernel, [((D, 512), BF16)], 1.1)(turned, turned_other, keep, received)
    pieces = lax.all_to_all(product.reshape(32, 32, 512), GRID, 0, 0)
    banded = jnp.sum(pieces.astype(F32), axis=0).astype(BF16)
    columns = jnp.transpose(banded.reshape(32, 4, 128), (1, 0, 2))
    last = lax.all_to_all(columns, "zh", 0, 0)
    grad_value = jnp.sum(last.astype(F32), axis=0)
    return crps_terms[None], grad_value


def solution(mesh):
    parts = Mesh(mesh.devices.reshape(4, 2, 4, 2, 4), ("zh", "core", "y", "zl", "x"))
    member = ("zh", "core")
    return jax.shard_map(
        body,
        mesh=parts,
        in_specs=(
            P(member, GRID, None), P(), P(), P(), P(), P(), P(), P(GRID), P(None, GRID),
        ),
        out_specs=(P(member, None, GRID), P(GRID, member)),
        check_vma=False,
    )
```

```python
import jax
import jax.numpy as jnp
from jax import lax
from jax.experimental import pallas as pl
from jax.experimental.pallas import tpu as pltpu
from jax.sharding import Mesh, PartitionSpec as P

F32 = jnp.float32
BF16 = jnp.bfloat16
ROWS = 256
REACH = 128
D = 1024
PAIRS = 8
PTS = 1024
CH = 128
MEMBERS = 8
BANDS = 32
MASKED = -1e30
GRID = ("y", "zl", "x")

NT = (((1,), (1,)), ((), ()))


def mm(a, b):
    return jnp.dot(a, b, preferred_element_type=F32)


def mm_nt(a, b):
    return lax.dot_general(a, b, NT, preferred_element_type=F32)


def rms(states, gain):
    floats = states.astype(F32)
    meansq = jnp.mean(floats * floats, axis=-1, keepdims=True) + 1e-05
    return (floats * lax.rsqrt(meansq) * gain).astype(BF16)


def thirds(values):
    first = values.astype(BF16)
    rest = values - first.astype(F32)
    second = rest.astype(BF16)
    third = (rest - second.astype(F32)).astype(BF16)
    return first, second, third


def call(kernel, outs, cost, scratch=(), hbm=0, limit=16, keep=False):
    def run(*args):
        args = [
            pltpu.with_memory_space_constraint(arg, pltpu.HBM) if i < hbm else arg
            for i, arg in enumerate(args)
        ]
        in_specs = [pl.BlockSpec(memory_space=pltpu.HBM)] * hbm
        in_specs += [pl.BlockSpec(memory_space=pltpu.VMEM)] * (len(args) - hbm)
        other = pltpu.VMEM if keep else jax.ShapeDtypeStruct
        return pl.pallas_call(
            kernel,
            out_shape=[other(s, d) for s, d in outs],
            in_specs=in_specs,
            out_specs=[pl.BlockSpec(memory_space=pltpu.VMEM)] * len(outs),
            scratch_shapes=list(scratch),
            compiler_params=pltpu.CompilerParams(vmem_limit_bytes=limit * 2**20),
            cost_estimate=pl.CostEstimate(
                flops=int(cost * 1e9), bytes_accessed=int(cost * 3e6), transcendentals=0
            ),
        )(*args)

    return run


def split_kernel(x_hbm, x_ref, up_ref, down_ref, sems):
    copies = [
        pltpu.make_async_copy(x_hbm.at[REACH:], up_ref, sems.at[0]),
        pltpu.make_async_copy(x_hbm.at[:REACH], down_ref, sems.at[1]),
        pltpu.make_async_copy(x_hbm, x_ref, sems.at[2]),
    ]
    for copy in copies:
        copy.start()
    for copy in copies:
        copy.wait()


def project_kernel(
    wq_hbm, wk_hbm, wv_hbm, wo_hbm, wd_hbm, gain_hbm, x_ref,
    q_ref, k_ref, vt_ref, n_ref, wk_ref, wv_ref, wo_ref, wd_ref, gain_ref, wq, sems,
):
    half = D // 2
    copies = [pltpu.make_async_copy(gain_hbm, gain_ref, sems.at[0])]
    for hbm, vmem in ((wq_hbm, wq), (wk_hbm, wk_ref), (wv_hbm, wv_ref), (wo_hbm, wo_ref)):
        for j in range(2):
            rows = slice(j * half, (j + 1) * half)
            copies.append(
                pltpu.make_async_copy(hbm.at[rows], vmem.at[rows], sems.at[len(copies)])
            )
    copies.append(pltpu.make_async_copy(wd_hbm, wd_ref, sems.at[len(copies)]))
    for copy in copies:
        copy.start()
    copies[0].wait()
    normed = rms(x_ref[...], gain_ref[...])
    n_ref[...] = normed
    copies[1].wait()
    copies[2].wait()
    q_ref[...] = mm(normed, wq[...]).astype(BF16) * jnp.asarray(0.125, BF16)
    copies[3].wait()
    copies[4].wait()
    k_ref[...] = mm(normed, wk_ref[...]).astype(BF16)
    copies[5].wait()
    copies[6].wait()
    vt_ref[...] = mm(normed, wv_ref[...]).T.astype(BF16)
    for copy in copies[7:]:
        copy.wait()


def attend_kernel(
    xb_ref, xa_ref, gain_ref, wk_ref, wv_ref, q_ref, k_ref, vt_ref, x_ref, wo_ref, wd_ref,
    probs, dec_ref, dech_ref, nh_ref, kh, vht, mixed,
):
    band = band_index()
    gain = gain_ref[...]
    nh_ref[:REACH] = rms(xb_ref[...], gain)
    nh_ref[REACH:] = rms(xa_ref[...], gain)
    halo = nh_ref[...]
    kh[...] = mm(halo, wk_ref[...]).astype(BF16)
    vht[...] = mm(halo, wv_ref[...]).T.astype(BF16)
    lane = lax.broadcasted_iota(jnp.int32, (REACH, 128), 1)
    low = (lane < 64).astype(F32).astype(BF16)
    high = (lane >= 64).astype(F32).astype(BF16)
    row_low = lax.broadcasted_iota(jnp.int32, (128, REACH), 0) < 64
    key = lax.broadcasted_iota(jnp.int32, (REACH, 2 * REACH), 0)
    query = lax.broadcasted_iota(jnp.int32, (REACH, 2 * REACH), 1) % REACH
    before = jnp.where(key <= query, 0.0, MASKED)
    after = jnp.where(key >= query, 0.0, MASKED)
    first = jnp.where((key >= query) & (band > 0), 0.0, MASKED)
    last = jnp.where((key <= query) & (band < BANDS - 1), 0.0, MASKED)
    for block in range(2):
        rows = slice(block * REACH, (block + 1) * REACH)
        for pair in range(PAIRS):
            cols = slice(pair * 128, (pair + 1) * 128)
            both = q_ref[rows, cols]
            stacked = jnp.concatenate([both * low, both * high], axis=0)
            s0 = mm_nt(k_ref[:REACH, cols], stacked)
            s1 = mm_nt(k_ref[REACH:, cols], stacked)
            s2 = mm_nt(kh[rows, cols], stacked)
            if block == 0:
                s1 += before
                s2 += first
            else:
                s0 += after
                s2 += last
            top = jnp.max(jnp.maximum(jnp.maximum(s0, s1), s2), axis=0, keepdims=True)
            e0 = jnp.exp(s0 - top)
            e1 = jnp.exp(s1 - top)
            e2 = jnp.exp(s2 - top)
            inv = 1.0 / jnp.sum(e0 + e1 + e2, axis=0, keepdims=True)
            po = jnp.concatenate([(e0 * inv).astype(BF16), (e1 * inv).astype(BF16)], axis=0)
            ph = (e2 * inv).astype(BF16)
            probs[pair, block, :ROWS] = po
            probs[pair, block, ROWS:] = ph
            out = mm(vt_ref[cols, :], po) + mm(vht[cols, rows], ph)
            out = jnp.where(row_low, out[:, :REACH], out[:, REACH:])
            mixed[rows, cols] = out.T.astype(BF16)
    projected = mm(mixed[...], wo_ref[...])
    hidden = (x_ref[...].astype(F32) + projected).astype(BF16)
    decoded = mm(hidden, wd_ref[...]).T
    dec_ref[...] = decoded
    dech_ref[...] = decoded.astype(BF16)


def band_index():
    return (lax.axis_index("y") * 2 + lax.axis_index("zl")) * 4 + lax.axis_index("x")


def selector(node_ref):
    node = lax.broadcasted_iota(jnp.int32, (ROWS, PTS), 0) + band_index() * ROWS
    return (node == node_ref[...]).astype(F32).astype(BF16)


def truth_kernel(
    dec_ref, node_ref, truth_ref, n_ref, nh_ref, abs_ref, slope_ref, count_ref, t_ref, own_ref
):
    t_ref[:, :ROWS] = n_ref[...].astype(F32).T.astype(BF16)
    t_ref[:, ROWS:] = nh_ref[...].astype(F32).T.astype(BF16)
    own_ref[...] = dec_ref[...].astype(BF16)
    select = selector(node_ref)
    parts = thirds(dec_ref[...])
    pred = mm(parts[2], select) + mm(parts[1], select) + mm(parts[0], select)
    error = pred - truth_ref[...]
    square = error * error + 0.25
    inverse = lax.rsqrt(square)
    abs_ref[...] = square * inverse
    slope = error * inverse
    high = slope.astype(BF16)
    rest = (slope - high.astype(F32)).astype(BF16)
    slope_ref[...] = mm_nt(high, select) + mm_nt(rest, select)
    count_ref[...] = mm_nt(jnp.ones((16, PTS), BF16), select)[:8]


def backward_kernel(
    probs, wd, wo, dec_ref, oz_ref, oc_ref, slope_ref, count_ref,
    keep_ref, send_ref, spread_ref, mg,
):
    own = dec_ref[...]
    spread = jnp.full((CH, ROWS), 0.5, F32)
    total = jnp.zeros((CH, ROWS), F32)
    for other in [oz_ref[i] for i in range(3)] + [oc_ref[i] for i in range(4)]:
        differ = own - other.astype(F32)
        square = differ * differ + 0.25
        inverse = lax.rsqrt(square)
        spread += square * inverse
        total += differ * inverse
    spread_ref[...] = spread
    node_grad = (slope_ref[...] - count_ref[:1] * total * (1.0 / (MEMBERS - 1))) * (1.0 / MEMBERS)
    high = node_grad.astype(BF16)
    rest = (node_grad - high.astype(F32)).astype(BF16)
    hidden_grad = (mm(wd[...], high) + mm(wd[...], rest)).astype(BF16)
    mg[...] = mm(wo[...], hidden_grad).astype(BF16)
    feature = lax.broadcasted_iota(jnp.int32, (128, REACH), 0)
    low = (feature < 64).astype(F32).astype(BF16)
    high_rows = (feature >= 64).astype(F32).astype(BF16)
    for which, out_ref in ((1, send_ref), (0, keep_ref)):
        for z in range(4):
            pair = 2 * z + (lax.axis_index("core") + which) % 2
            grads = mg[pl.ds(pl.multiple_of(pair * 128, 128), 128), :]
            rows = slice(z * 128, (z + 1) * 128)
            total = None
            for block in range(2):
                part = grads[:, block * REACH : (block + 1) * REACH]
                both = jnp.concatenate([part * low, part * high_rows], axis=1)
                term = mm_nt(both, probs[pair, block, :ROWS])
                total = term if block == 0 else total + term
                edge = slice(ROWS + block * REACH, ROWS + (block + 1) * REACH)
                out_ref[rows, edge] = mm_nt(both, probs[pair, block, ROWS:]).astype(BF16)
            out_ref[rows, :ROWS] = total.astype(BF16)


def product_kernel(t_ref, u_ref, keep_ref, recv_ref, out_ref):
    out_ref[...] = (
        mm_nt(t_ref[...], keep_ref[...]) + mm_nt(u_ref[...], recv_ref[...])
    ).astype(BF16)


def band_kernel(pieces_ref, *rest):
    outs, total = rest[:4], rest[4]
    both = pieces_ref[0].astype(F32)
    for i in range(1, 32):
        both += pieces_ref[i].astype(F32)
    for i in range(4):
        total[i] = both[:, i * 128 : (i + 1) * 128]
    for k in range(4):
        outs[k][...] = total[(lax.axis_index("zh") + k) % 4].astype(BF16)


def stack_kernel(a_ref, b_ref, c_ref, d_ref, out_ref):
    for i, ref in enumerate((a_ref, b_ref, c_ref, d_ref)):
        out_ref[i] = ref[...]


def last_kernel(a_ref, b_ref, c_ref, d_ref, out_ref):
    out_ref[...] = (a_ref[...].astype(F32) + b_ref[...].astype(F32)) + (
        c_ref[...].astype(F32) + d_ref[...].astype(F32)
    )


def crps_kernel(abs_ref, spread_ref, node_ref, out_ref):
    select = selector(node_ref)
    parts = thirds(spread_ref[...])
    spread = mm(parts[2], select) + mm(parts[1], select) + mm(parts[0], select)
    out_ref[...] = abs_ref[...] - spread * (1.0 / (2.0 * (MEMBERS - 1)))


def ring(chunks, axis):
    return [chunks[0]] + [
        lax.ppermute(chunks[k], axis, [(i, (i + k) % 4) for i in range(4)]) for k in (2, 1, 3)
    ]


def body(inputs, norm_gain, w_query, w_key, w_value, w_out, w_decode, point_node, truth):
    states = inputs[0]
    gain = norm_gain[None]
    node = point_node[None]
    up = [(i, i + 1) for i in range(BANDS - 1)]
    down = [(i + 1, i) for i in range(BANDS - 1)]
    swap = [(0, 1), (1, 0)]
    half = ((REACH, D), BF16)
    wide = ((ROWS, D), BF16)
    matrix = ((D, D), BF16)
    here, upper, lower = call(
        split_kernel, [wide, half, half], 0.2, [pltpu.SemaphoreType.DMA((3,))], hbm=1, keep=True
    )(states)
    before = lax.ppermute(upper, GRID, up)
    after = lax.ppermute(lower, GRID, down)
    queries, keys, values, normed, w_key, w_value, w_out, w_decode, gain = call(
        project_kernel,
        [wide, wide, ((D, ROWS), BF16), wide, matrix, matrix, matrix, ((D, CH), BF16), ((1, D), F32)],
        1.6,
        [pltpu.VMEM((D, D), BF16), pltpu.SemaphoreType.DMA((10,))],
        hbm=6,
        keep=True,
    )(w_query, w_key, w_value, w_out, w_decode, gain, here)
    probs, decoded, decoded_half, normed_halo = call(
        attend_kernel,
        [((PAIRS, 2, ROWS + REACH, 2 * REACH), BF16), ((CH, ROWS), F32), ((CH, ROWS), BF16), wide],
        4.0,
        [pltpu.VMEM((ROWS, D), BF16), pltpu.VMEM((D, ROWS), BF16), pltpu.VMEM((ROWS, D), BF16)],
        limit=20,
        keep=True,
    )(before, after, gain, w_key, w_value, queries, keys, values, here, w_out, w_decode)
    along = ring([None, decoded_half, decoded_half, decoded_half], "zh")[1:]
    abs_error, slope, count, turned, own = call(
        truth_kernel,
        [((CH, PTS), F32), ((CH, ROWS), F32), ((8, ROWS), F32), ((D, 2 * ROWS), BF16)]
        + [((CH, ROWS), BF16)],
        2.0,
    )(decoded, node, truth, normed, normed_halo)
    (along,) = call(stack_kernel, [((4, CH, ROWS), BF16)], 0.1)(*along, own)
    across = lax.ppermute(along, "core", swap)
    turned_other = lax.ppermute(turned, "core", swap)
    square = ((512, 512), BF16)
    keep, send, spread = call(
        backward_kernel, [square, square, ((CH, ROWS), F32)], 3.0, [pltpu.VMEM((D, ROWS), BF16)]
    )(probs, w_decode, w_out, decoded, along, across, slope, count)
    received = lax.ppermute(send, "core", swap)
    (product,) = call(product_kernel, [((D, 512), BF16)], 1.1)(turned, turned_other, keep, received)
    pieces = lax.all_to_all(product.reshape(32, 32, 512), GRID, 0, 0)
    columns = call(
        band_kernel, [((32, 128), BF16)] * 4, 0.1, [pltpu.VMEM((4, 32, 128), F32)]
    )(pieces)
    columns = ring(columns, "zh")
    (crps_terms,) = call(crps_kernel, [((CH, PTS), F32)], 1.0)(abs_error, spread, node)
    (grad_value,) = call(last_kernel, [((32, 128), F32)], 0.1)(*columns)
    return crps_terms[None], grad_value


def solution(mesh):
    parts = Mesh(mesh.devices.reshape(4, 2, 4, 2, 4), ("zh", "core", "y", "zl", "x"))
    member = ("zh", "core")
    return jax.shard_map(
        body,
        mesh=parts,
        in_specs=(
            P(member, GRID, None), P(), P(), P(), P(), P(), P(), P(GRID), P(None, GRID),
        ),
        out_specs=(P(member, None, GRID), P(GRID, member)),
        check_vma=False,
    )
```

```python
import jax
import jax.numpy as jnp
from jax import lax
from jax.experimental import pallas as pl
from jax.experimental.pallas import tpu as pltpu
from jax.sharding import Mesh, PartitionSpec as P

F32 = jnp.float32
BF16 = jnp.bfloat16
ROWS = 256
REACH = 128
D = 1024
PAIRS = 8
PTS = 1024
CH = 128
MEMBERS = 8
BANDS = 32
MASKED = -1e30
GRID = ("y", "zl", "x")

NT = (((1,), (1,)), ((), ()))


def mm(a, b):
    return jnp.dot(a, b, preferred_element_type=F32)


def mm_nt(a, b):
    return lax.dot_general(a, b, NT, preferred_element_type=F32)


def rms(states, gain):
    floats = states.astype(F32)
    meansq = jnp.mean(floats * floats, axis=-1, keepdims=True) + 1e-05
    return (floats * lax.rsqrt(meansq) * gain).astype(BF16)


def thirds(values):
    first = values.astype(BF16)
    rest = values - first.astype(F32)
    second = rest.astype(BF16)
    third = (rest - second.astype(F32)).astype(BF16)
    return first, second, third


def call(kernel, outs, cost, scratch=(), hbm=0, limit=16, keep=False):
    def run(*args):
        args = [
            pltpu.with_memory_space_constraint(arg, pltpu.HBM) if i < hbm else arg
            for i, arg in enumerate(args)
        ]
        in_specs = [pl.BlockSpec(memory_space=pltpu.HBM)] * hbm
        in_specs += [pl.BlockSpec(memory_space=pltpu.VMEM)] * (len(args) - hbm)
        other = pltpu.VMEM if keep else jax.ShapeDtypeStruct
        return pl.pallas_call(
            kernel,
            out_shape=[other(s, d) for s, d in outs],
            in_specs=in_specs,
            out_specs=[pl.BlockSpec(memory_space=pltpu.VMEM)] * len(outs),
            scratch_shapes=list(scratch),
            compiler_params=pltpu.CompilerParams(vmem_limit_bytes=limit * 2**20),
            cost_estimate=pl.CostEstimate(
                flops=int(cost * 1e9), bytes_accessed=int(cost * 3e6), transcendentals=0
            ),
        )(*args)

    return run


def split_kernel(x_hbm, up_ref, down_ref, sems):
    copies = [
        pltpu.make_async_copy(x_hbm.at[REACH:], up_ref, sems.at[0]),
        pltpu.make_async_copy(x_hbm.at[:REACH], down_ref, sems.at[1]),
    ]
    for copy in copies:
        copy.start()
    for copy in copies:
        copy.wait()


def head_parts():
    lane = lax.broadcasted_iota(jnp.int32, (REACH, 128), 1)
    low = (lane < 64).astype(F32).astype(BF16)
    high = (lane >= 64).astype(F32).astype(BF16)
    row_low = lax.broadcasted_iota(jnp.int32, (128, REACH), 0) < 64
    key = lax.broadcasted_iota(jnp.int32, (REACH, 2 * REACH), 0)
    query = lax.broadcasted_iota(jnp.int32, (REACH, 2 * REACH), 1) % REACH
    return low, high, row_low, key, query


def project_kernel(
    wq_hbm, wk_hbm, wv_hbm, wo_hbm, wd_hbm, gain_hbm, x_hbm,
    q_ref, n_ref, x_ref, wk_ref, wv_ref, wo_ref, wd_ref, gain_ref, e_ref, out_ref, top_ref, sum_ref,
    wq, k, vt, sems,
):
    half = D // 2
    copies = [pltpu.make_async_copy(x_hbm, x_ref, sems.at[0])]
    copies.append(pltpu.make_async_copy(gain_hbm, gain_ref, sems.at[1]))
    for hbm, vmem in ((wq_hbm, wq), (wk_hbm, wk_ref), (wv_hbm, wv_ref), (wo_hbm, wo_ref)):
        for j in range(2):
            rows = slice(j * half, (j + 1) * half)
            copies.append(
                pltpu.make_async_copy(hbm.at[rows], vmem.at[rows], sems.at[len(copies)])
            )
    copies.append(pltpu.make_async_copy(wd_hbm, wd_ref, sems.at[len(copies)]))
    for copy in copies:
        copy.start()
    copies[0].wait()
    copies[1].wait()
    normed = rms(x_ref[...], gain_ref[...])
    n_ref[...] = normed
    copies[2].wait()
    copies[3].wait()
    q_ref[...] = mm(normed, wq[...]).astype(BF16) * jnp.asarray(0.125, BF16)
    copies[4].wait()
    copies[5].wait()
    k[...] = mm(normed, wk_ref[...]).astype(BF16)
    copies[6].wait()
    copies[7].wait()
    vt[...] = mm(normed, wv_ref[...]).T.astype(BF16)
    low, high, row_low, key, query = head_parts()
    before = jnp.where(key <= query, 0.0, MASKED)
    after = jnp.where(key >= query, 0.0, MASKED)
    for block in range(2):
        rows = slice(block * REACH, (block + 1) * REACH)
        for pair in range(PAIRS):
            cols = slice(pair * 128, (pair + 1) * 128)
            both = q_ref[rows, cols]
            stacked = jnp.concatenate([both * low, both * high], axis=0)
            s0 = mm_nt(k[:REACH, cols], stacked)
            s1 = mm_nt(k[REACH:, cols], stacked)
            if block == 0:
                s1 += before
            else:
                s0 += after
            top = jnp.max(jnp.maximum(s0, s1), axis=0, keepdims=True)
            e0 = jnp.exp(s0 - top)
            e1 = jnp.exp(s1 - top)
            n = pair * 2 + block
            top_ref[n : n + 1] = top
            sum_ref[n : n + 1] = jnp.sum(e0 + e1, axis=0, keepdims=True)
            e = jnp.concatenate([e0.astype(BF16), e1.astype(BF16)], axis=0)
            e_ref[pair, block] = e
            out = mm(vt[cols, :], e)
            out_ref[pair, block] = jnp.where(row_low, out[:, :REACH], out[:, REACH:])
    for copy in copies[8:]:
        copy.wait()


def attend_kernel(
    xb_ref, xa_ref, gain_ref, wk_ref, wv_ref, q_ref, out_ref, top_ref, sum_ref, x_ref, wo_ref, wd_ref,
    e_ref, factor_ref, dec_ref, dech_ref, nh_ref, kh, vht, mixed,
):
    band = band_index()
    gain = gain_ref[...]
    nh_ref[:REACH] = rms(xb_ref[...], gain)
    nh_ref[REACH:] = rms(xa_ref[...], gain)
    halo = nh_ref[...]
    kh[...] = mm(halo, wk_ref[...]).astype(BF16)
    vht[...] = mm(halo, wv_ref[...]).T.astype(BF16)
    low, high, row_low, key, query = head_parts()
    first = jnp.where((key >= query) & (band > 0), 0.0, MASKED)
    last = jnp.where((key <= query) & (band < BANDS - 1), 0.0, MASKED)
    for block in range(2):
        rows = slice(block * REACH, (block + 1) * REACH)
        for pair in range(PAIRS):
            cols = slice(pair * 128, (pair + 1) * 128)
            both = q_ref[rows, cols]
            stacked = jnp.concatenate([both * low, both * high], axis=0)
            scores = mm_nt(kh[rows, cols], stacked) + (last if block else first)
            n = pair * 2 + block
            top_own = top_ref[n : n + 1]
            top_halo = jnp.max(scores, axis=0, keepdims=True)
            e = jnp.exp(scores - top_halo)
            e_ref[pair, block] = e.astype(BF16)
            top = jnp.maximum(top_own, top_halo)
            scale_own = jnp.exp(top_own - top)
            scale_halo = jnp.exp(top_halo - top)
            inv = 1.0 / (
                sum_ref[n : n + 1] * scale_own + jnp.sum(e, axis=0, keepdims=True) * scale_halo
            )
            scale_own *= inv
            scale_halo *= inv
            factor_ref[pair, 2 * block : 2 * block + 1] = scale_own
            factor_ref[pair, 2 * block + 1 : 2 * block + 2] = scale_halo
            out = mm(vht[cols, rows], e.astype(BF16)) * scale_halo
            out = jnp.where(row_low, out[:, :REACH], out[:, REACH:])
            out += out_ref[pair, block] * jnp.where(
                row_low, scale_own[:, :REACH], scale_own[:, REACH:]
            )
            mixed[rows, cols] = out.T.astype(BF16)
    projected = mm(mixed[...], wo_ref[...])
    hidden = (x_ref[...].astype(F32) + projected).astype(BF16)
    decoded = mm(hidden, wd_ref[...]).T
    dec_ref[...] = decoded
    dech_ref[...] = decoded.astype(BF16)


def band_index():
    return (lax.axis_index("y") * 2 + lax.axis_index("zl")) * 4 + lax.axis_index("x")


def selector(node_ref):
    node = lax.broadcasted_iota(jnp.int32, (ROWS, PTS), 0) + band_index() * ROWS
    return (node == node_ref[...]).astype(F32).astype(BF16)


def truth_kernel(
    dec_ref, node_ref, truth_ref, n_ref, nh_ref, abs_ref, slope_ref, count_ref, t_ref, own_ref
):
    t_ref[:, :ROWS] = n_ref[...].astype(F32).T.astype(BF16)
    t_ref[:, ROWS:] = nh_ref[...].astype(F32).T.astype(BF16)
    own_ref[...] = dec_ref[...].astype(BF16)
    select = selector(node_ref)
    parts = thirds(dec_ref[...])
    pred = mm(parts[2], select) + mm(parts[1], select) + mm(parts[0], select)
    error = pred - truth_ref[...]
    square = error * error + 0.25
    inverse = lax.rsqrt(square)
    abs_ref[...] = square * inverse
    slope = error * inverse
    high = slope.astype(BF16)
    rest = (slope - high.astype(F32)).astype(BF16)
    slope_ref[...] = mm_nt(high, select) + mm_nt(rest, select)
    count_ref[...] = mm_nt(jnp.ones((16, PTS), BF16), select)[:8]


def backward_kernel(
    eo_ref, eh_ref, factor_ref, wd, wo, dec_ref, oz_ref, oc_ref, slope_ref, count_ref,
    keep_ref, send_ref, spread_ref, mg,
):
    own = dec_ref[...]
    spread = jnp.full((CH, ROWS), 0.5, F32)
    total = jnp.zeros((CH, ROWS), F32)
    for other in [oz_ref[i] for i in range(3)] + [oc_ref[i] for i in range(4)]:
        differ = own - other.astype(F32)
        square = differ * differ + 0.25
        inverse = lax.rsqrt(square)
        spread += square * inverse
        total += differ * inverse
    spread_ref[...] = spread
    node_grad = (slope_ref[...] - count_ref[:1] * total * (1.0 / (MEMBERS - 1))) * (1.0 / MEMBERS)
    high = node_grad.astype(BF16)
    rest = (node_grad - high.astype(F32)).astype(BF16)
    hidden_grad = (mm(wd[...], high) + mm(wd[...], rest)).astype(BF16)
    mg[...] = mm(wo[...], hidden_grad).astype(BF16)
    feature = lax.broadcasted_iota(jnp.int32, (128, 2 * REACH), 0)
    lane = lax.broadcasted_iota(jnp.int32, (128, 2 * REACH), 1)
    heads = ((feature < 64) == (lane < REACH)).astype(F32)
    for which, out_ref in ((1, send_ref), (0, keep_ref)):
        for z in range(4):
            pair = 2 * z + (lax.axis_index("core") + which) % 2
            grads = mg[pl.ds(pl.multiple_of(pair * 128, 128), 128), :].astype(F32)
            rows = slice(z * 128, (z + 1) * 128)
            total = None
            for block in range(2):
                part = grads[:, block * REACH : (block + 1) * REACH]
                both = jnp.concatenate([part, part], axis=1) * heads
                factors = factor_ref[pair]
                own = (both * factors[2 * block : 2 * block + 1]).astype(BF16)
                halo = (both * factors[2 * block + 1 : 2 * block + 2]).astype(BF16)
                term = mm_nt(own, eo_ref[pair, block])
                total = term if block == 0 else total + term
                edge = slice(ROWS + block * REACH, ROWS + (block + 1) * REACH)
                out_ref[rows, edge] = mm_nt(halo, eh_ref[pair, block]).astype(BF16)
            out_ref[rows, :ROWS] = total.astype(BF16)


def product_kernel(t_ref, u_ref, keep_ref, recv_ref, out_ref):
    out_ref[...] = (
        mm_nt(t_ref[...], keep_ref[...]) + mm_nt(u_ref[...], recv_ref[...])
    ).astype(BF16)


def band_kernel(pieces_ref, *rest):
    outs, total = rest[:4], rest[4]
    both = pieces_ref[0].astype(F32)
    for i in range(1, 32):
        both += pieces_ref[i].astype(F32)
    for i in range(4):
        total[i] = both[:, i * 128 : (i + 1) * 128]
    for k in range(4):
        outs[k][...] = total[(lax.axis_index("zh") + k) % 4].astype(BF16)


def stack_kernel(a_ref, b_ref, c_ref, d_ref, out_ref):
    for i, ref in enumerate((a_ref, b_ref, c_ref, d_ref)):
        out_ref[i] = ref[...]


def last_kernel(a_ref, b_ref, c_ref, d_ref, out_ref):
    out_ref[...] = (a_ref[...].astype(F32) + b_ref[...].astype(F32)) + (
        c_ref[...].astype(F32) + d_ref[...].astype(F32)
    )


def crps_kernel(abs_ref, spread_ref, node_ref, out_ref):
    select = selector(node_ref)
    parts = thirds(spread_ref[...])
    spread = mm(parts[2], select) + mm(parts[1], select) + mm(parts[0], select)
    out_ref[...] = abs_ref[...] - spread * (1.0 / (2.0 * (MEMBERS - 1)))


def ring(chunks, axis):
    return [chunks[0]] + [
        lax.ppermute(chunks[k], axis, [(i, (i + k) % 4) for i in range(4)]) for k in (2, 1, 3)
    ]


def body(inputs, norm_gain, w_query, w_key, w_value, w_out, w_decode, point_node, truth):
    states = inputs[0]
    gain = norm_gain[None]
    node = point_node[None]
    up = [(i, i + 1) for i in range(BANDS - 1)]
    down = [(i + 1, i) for i in range(BANDS - 1)]
    swap = [(0, 1), (1, 0)]
    half = ((REACH, D), BF16)
    wide = ((ROWS, D), BF16)
    matrix = ((D, D), BF16)
    row = ((2 * PAIRS, 2 * REACH), F32)
    upper, lower = call(
        split_kernel, [half, half], 0.2, [pltpu.SemaphoreType.DMA((2,))], hbm=1, keep=True
    )(states)
    before = lax.ppermute(upper, GRID, up)
    after = lax.ppermute(lower, GRID, down)
    (
        queries, normed, here, w_key, w_value, w_out, w_decode, gain, exp_own, mixed_own, top_own,
        sum_own,
    ) = call(
        project_kernel,
        [wide, wide, wide, matrix, matrix, matrix, ((D, CH), BF16), ((1, D), F32)]
        + [((PAIRS, 2, ROWS, 2 * REACH), BF16), ((PAIRS, 2, 128, REACH), F32), row, row],
        3.0,
        [
            pltpu.VMEM((D, D), BF16),
            pltpu.VMEM((ROWS, D), BF16),
            pltpu.VMEM((D, ROWS), BF16),
            pltpu.SemaphoreType.DMA((11,)),
        ],
        hbm=7,
        limit=20,
        keep=True,
    )(w_query, w_key, w_value, w_out, w_decode, gain, states)
    exp_halo, factors, decoded, decoded_half, normed_halo = call(
        attend_kernel,
        [((PAIRS, 2, REACH, 2 * REACH), BF16), ((PAIRS, 4, 2 * REACH), F32)]
        + [((CH, ROWS), F32), ((CH, ROWS), BF16), wide],
        3.0,
        [pltpu.VMEM((ROWS, D), BF16), pltpu.VMEM((D, ROWS), BF16), pltpu.VMEM((ROWS, D), BF16)],
        limit=20,
        keep=True,
    )(
        before, after, gain, w_key, w_value, queries, mixed_own, top_own, sum_own, here, w_out,
        w_decode,
    )
    along = ring([None, decoded_half, decoded_half, decoded_half], "zh")[1:]
    abs_error, slope, count, turned, own = call(
        truth_kernel,
        [((CH, PTS), F32), ((CH, ROWS), F32), ((8, ROWS), F32), ((D, 2 * ROWS), BF16)]
        + [((CH, ROWS), BF16)],
        2.0,
    )(decoded, node, truth, normed, normed_halo)
    (along,) = call(stack_kernel, [((4, CH, ROWS), BF16)], 0.1)(*along, own)
    across = lax.ppermute(along, "core", swap)
    turned_other = lax.ppermute(turned, "core", swap)
    square = ((512, 512), BF16)
    keep, send, spread = call(
        backward_kernel, [square, square, ((CH, ROWS), F32)], 3.0, [pltpu.VMEM((D, ROWS), BF16)]
    )(exp_own, exp_halo, factors, w_decode, w_out, decoded, along, across, slope, count)
    received = lax.ppermute(send, "core", swap)
    (product,) = call(product_kernel, [((D, 512), BF16)], 1.1)(turned, turned_other, keep, received)
    pieces = lax.all_to_all(product.reshape(32, 32, 512), GRID, 0, 0)
    columns = call(
        band_kernel, [((32, 128), BF16)] * 4, 0.1, [pltpu.VMEM((4, 32, 128), F32)]
    )(pieces)
    columns = ring(columns, "zh")
    (crps_terms,) = call(crps_kernel, [((CH, PTS), F32)], 1.0)(abs_error, spread, node)
    (grad_value,) = call(last_kernel, [((32, 128), F32)], 0.1)(*columns)
    return crps_terms[None], grad_value


def solution(mesh):
    parts = Mesh(mesh.devices.reshape(4, 2, 4, 2, 4), ("zh", "core", "y", "zl", "x"))
    member = ("zh", "core")
    return jax.shard_map(
        body,
        mesh=parts,
        in_specs=(
            P(member, GRID, None), P(), P(), P(), P(), P(), P(), P(GRID), P(None, GRID),
        ),
        out_specs=(P(member, None, GRID), P(GRID, member)),
        check_vma=False,
    )
```

```python
import jax
import jax.numpy as jnp
import numpy as np
from jax import lax
from jax.experimental import pallas as pl
from jax.experimental.pallas import tpu as pltpu
from jax.sharding import Mesh, PartitionSpec as P

F32 = jnp.float32
BF16 = jnp.bfloat16
ROWS = 256
REACH = 128
D = 1024
PAIRS = 8
PTS = 1024
CH = 128
MEMBERS = 8
BANDS = 32
OWN_GAP = 4
HALO_GAP = 4
BACK_GAP = 2
MASKED = -1e30
GRID = ("y", "zl", "x")

NT = (((1,), (1,)), ((), ()))


def mm(a, b):
    return jnp.dot(a, b, preferred_element_type=F32)


def mm_nt(a, b):
    return lax.dot_general(a, b, NT, preferred_element_type=F32)


def rms(states, gain):
    floats = states.astype(F32)
    meansq = jnp.mean(floats * floats, axis=-1, keepdims=True) + 1e-05
    return (floats * lax.rsqrt(meansq) * gain).astype(BF16)


def thirds(values):
    first = values.astype(BF16)
    rest = values - first.astype(F32)
    second = rest.astype(BF16)
    third = (rest - second.astype(F32)).astype(BF16)
    return first, second, third


def call(kernel, outs, cost, scratch=(), hbm=0, limit=16, keep=False):
    def run(*args):
        args = [
            pltpu.with_memory_space_constraint(arg, pltpu.HBM) if i < hbm else arg
            for i, arg in enumerate(args)
        ]
        in_specs = [pl.BlockSpec(memory_space=pltpu.HBM)] * hbm
        in_specs += [pl.BlockSpec(memory_space=pltpu.VMEM)] * (len(args) - hbm)
        other = pltpu.VMEM if keep else jax.ShapeDtypeStruct
        return pl.pallas_call(
            kernel,
            out_shape=[other(s, d) for s, d in outs],
            in_specs=in_specs,
            out_specs=[pl.BlockSpec(memory_space=pltpu.VMEM)] * len(outs),
            scratch_shapes=list(scratch),
            compiler_params=pltpu.CompilerParams(vmem_limit_bytes=limit * 2**20),
            cost_estimate=pl.CostEstimate(
                flops=int(cost * 1e9), bytes_accessed=int(cost * 3e6), transcendentals=0
            ),
        )(*args)

    return run


def split_kernel(x_hbm, first_ref, second_ref, sems):
    core = lax.axis_index("core")
    copies = [
        pltpu.make_async_copy(
            x_hbm.at[pl.ds(pl.multiple_of(start * REACH, REACH), REACH)], ref, sems.at[i]
        )
        for i, (start, ref) in enumerate(((1 - core, first_ref), (core, second_ref)))
    ]
    for copy in copies:
        copy.start()
    for copy in copies:
        copy.wait()


def staged(items, stages, gap):
    kept = [(item,) for item in items]
    for step in range(len(items) + gap * (len(stages) - 1)):
        for s, stage in enumerate(stages):
            i = step - gap * s
            if 0 <= i < len(items):
                kept[i] = (items[i], *stage(*kept[i]))


BLOCKS = [(pair, block) for block in range(2) for pair in range(PAIRS)]


def head_parts():
    lane = lax.broadcasted_iota(jnp.int32, (REACH, 128), 1)
    low = (lane < 64).astype(F32).astype(BF16)
    high = (lane >= 64).astype(F32).astype(BF16)
    row_low = lax.broadcasted_iota(jnp.int32, (128, REACH), 0) < 64
    key = lax.broadcasted_iota(jnp.int32, (REACH, 2 * REACH), 0)
    query = lax.broadcasted_iota(jnp.int32, (REACH, 2 * REACH), 1) % REACH
    return low, high, row_low, key, query


def project_kernel(
    wq_hbm, wk_hbm, wv_hbm, wo_hbm, wd_hbm, gain_hbm, x_hbm,
    q_ref, n_ref, x_ref, wk_ref, wv_ref, wo_ref, wd_ref, gain_ref, e_ref, out_ref, top_ref, sum_ref,
    wq, k, vt, sems,
):
    half = D // 2
    copies = [pltpu.make_async_copy(x_hbm, x_ref, sems.at[0])]
    copies.append(pltpu.make_async_copy(gain_hbm, gain_ref, sems.at[1]))
    for hbm, vmem in ((wq_hbm, wq), (wk_hbm, wk_ref), (wv_hbm, wv_ref), (wo_hbm, wo_ref)):
        for j in range(2):
            rows = slice(j * half, (j + 1) * half)
            copies.append(
                pltpu.make_async_copy(hbm.at[rows], vmem.at[rows], sems.at[len(copies)])
            )
    copies.append(pltpu.make_async_copy(wd_hbm, wd_ref, sems.at[len(copies)]))
    for copy in copies:
        copy.start()
    copies[0].wait()
    copies[1].wait()
    normed = rms(x_ref[...], gain_ref[...])
    n_ref[...] = normed
    copies[2].wait()
    copies[3].wait()
    q_ref[...] = mm(normed, wq[...]).astype(BF16) * jnp.asarray(0.125, BF16)
    copies[4].wait()
    copies[5].wait()
    k[...] = mm(normed, wk_ref[...]).astype(BF16)
    copies[6].wait()
    copies[7].wait()
    vt[...] = mm(normed, wv_ref[...]).T.astype(BF16)
    low, high, row_low, key, query = head_parts()
    before = jnp.where(key <= query, 0.0, MASKED)
    after = jnp.where(key >= query, 0.0, MASKED)

    def scores(item):
        pair, block = item
        cols = slice(pair * 128, (pair + 1) * 128)
        both = q_ref[block * REACH : (block + 1) * REACH, cols]
        stacked = jnp.concatenate([both * low, both * high], axis=0)
        s0 = mm_nt(k[:REACH, cols], stacked)
        s1 = mm_nt(k[REACH:, cols], stacked)
        return (s0, s1 + before) if block == 0 else (s0 + after, s1)

    def softmax(item, s0, s1):
        pair, block = item
        n = pair * 2 + block
        top = jnp.max(jnp.maximum(s0, s1), axis=0, keepdims=True)
        e0 = jnp.exp(s0 - top)
        e1 = jnp.exp(s1 - top)
        top_ref[n : n + 1] = top
        sum_ref[n : n + 1] = jnp.sum(e0 + e1, axis=0, keepdims=True)
        e = jnp.concatenate([e0.astype(BF16), e1.astype(BF16)], axis=0)
        e_ref[pair, block] = e
        return (mm(vt[pair * 128 : (pair + 1) * 128, :], e),)

    def store(item, out):
        out_ref[item] = jnp.where(row_low, out[:, :REACH], out[:, REACH:])
        return ()

    staged(BLOCKS, (scores, softmax, store), OWN_GAP)
    for copy in copies[8:]:
        copy.wait()


def attend_kernel(
    first_ref, second_ref, gain_ref, wk_ref, wv_ref, q_ref, out_ref, top_ref, sum_ref, x_ref, wo_ref, wd_ref,
    e_ref, factor_ref, dec_ref, dech_ref, nh_ref, kh, vht, mixed,
):
    band = band_index()
    gain = gain_ref[...]
    core = lax.axis_index("core")
    for start, ref in ((core, first_ref), (1 - core, second_ref)):
        nh_ref[pl.ds(pl.multiple_of(start * REACH, REACH), REACH)] = rms(ref[...], gain)
    halo = nh_ref[...]
    kh[...] = mm(halo, wk_ref[...]).astype(BF16)
    vht[...] = mm(halo, wv_ref[...]).T.astype(BF16)
    low, high, row_low, key, query = head_parts()
    first = jnp.where((key >= query) & (band > 0), 0.0, MASKED)
    last = jnp.where((key <= query) & (band < BANDS - 1), 0.0, MASKED)

    def scores(item):
        pair, block = item
        rows = slice(block * REACH, (block + 1) * REACH)
        cols = slice(pair * 128, (pair + 1) * 128)
        both = q_ref[rows, cols]
        stacked = jnp.concatenate([both * low, both * high], axis=0)
        return (mm_nt(kh[rows, cols], stacked) + (last if block else first),)

    def softmax(item, scores):
        pair, block = item
        n = pair * 2 + block
        top_own = top_ref[n : n + 1]
        top_halo = jnp.max(scores, axis=0, keepdims=True)
        e = jnp.exp(scores - top_halo)
        e_half = e.astype(BF16)
        e_ref[pair, block] = e_half
        top = jnp.maximum(top_own, top_halo)
        scale_own = jnp.exp(top_own - top)
        scale_halo = jnp.exp(top_halo - top)
        inv = 1.0 / (
            sum_ref[n : n + 1] * scale_own + jnp.sum(e, axis=0, keepdims=True) * scale_halo
        )
        scale_own *= inv
        scale_halo *= inv
        factor_ref[pair, 2 * block : 2 * block + 1] = scale_own
        factor_ref[pair, 2 * block + 1 : 2 * block + 2] = scale_halo
        cols = slice(pair * 128, (pair + 1) * 128)
        out = mm(vht[cols, block * REACH : (block + 1) * REACH], e_half)
        return out, scale_own, scale_halo

    def join(item, out, scale_own, scale_halo):
        pair, block = item
        out *= scale_halo
        out = jnp.where(row_low, out[:, :REACH], out[:, REACH:])
        own = jnp.where(row_low, scale_own[:, :REACH], scale_own[:, REACH:])
        out += out_ref[pair, block] * own
        cols = slice(pair * 128, (pair + 1) * 128)
        mixed[block * REACH : (block + 1) * REACH, cols] = out.T.astype(BF16)
        return ()

    staged(BLOCKS, (scores, softmax, join), HALO_GAP)
    projected = mm(mixed[...], wo_ref[...])
    hidden = (x_ref[...].astype(F32) + projected).astype(BF16)
    decoded = mm(hidden, wd_ref[...]).T
    dec_ref[...] = decoded
    dech_ref[...] = decoded.astype(BF16)


def band_index():
    return (lax.axis_index("y") * 2 + lax.axis_index("zl")) * 4 + lax.axis_index("x")


def selector(node_ref):
    node = lax.broadcasted_iota(jnp.int32, (ROWS, PTS), 0) + band_index() * ROWS
    return (node == node_ref[...]).astype(F32).astype(BF16)


def truth_kernel(
    dec_ref, node_ref, truth_ref, n_ref, nh_ref, eo_ref, eh_ref, factor_ref,
    abs_ref, slope_ref, count_ref, keep_ref, send_ref, own_ref, po_ref, ph_ref,
):
    own_ref[...] = dec_ref[...].astype(BF16)
    select = selector(node_ref)
    parts = thirds(dec_ref[...])
    pred = mm(parts[2], select) + mm(parts[1], select) + mm(parts[0], select)
    error = pred - truth_ref[...]
    square = error * error + 0.25
    inverse = lax.rsqrt(square)
    abs_ref[...] = square * inverse
    slope = error * inverse
    high = slope.astype(BF16)
    rest = (slope - high.astype(F32)).astype(BF16)
    slope_ref[...] = mm_nt(high, select) + mm_nt(rest, select)
    count_ref[...] = mm_nt(jnp.ones((16, PTS), BF16), select)[:8]
    core = lax.axis_index("core")
    for columns, ref in ((slice(0, ROWS), n_ref), (slice(ROWS, 2 * ROWS), nh_ref)):
        for g in range(BANDS):
            rows = ref[:, g * 32 : (g + 1) * 32].astype(F32).T.astype(BF16)
            by_x = g % 4 * 8 + g // 4
            for which, out_ref in ((core, keep_ref), (1 - core, send_ref)):
                start = pl.multiple_of(jnp.where(which == 0, by_x, g) * 32, 32)
                out_ref[pl.ds(start, 32), columns] = rows
    for pair in range(PAIRS):
        for block in range(2):
            factors = factor_ref[pair]
            own = eo_ref[pair, block].astype(F32) * factors[2 * block : 2 * block + 1]
            po_ref[pair, block] = own.astype(BF16)
            halo = eh_ref[pair, block].astype(F32) * factors[2 * block + 1 : 2 * block + 2]
            ph_ref[pair, block] = halo.astype(BF16)


def value_terms(which, hidden_grad, wo_ref, po_ref, ph_ref, out_ref):
    core = lax.axis_index("core")
    pairs = [2 * z + (core + which) % 2 for z in range(4)]
    rows = [wo_ref[pl.ds(pl.multiple_of(pair * 128, 128), 128), :] for pair in pairs]
    mixed_grad = mm(jnp.concatenate(rows, axis=0), hidden_grad).astype(BF16)
    feature = lax.broadcasted_iota(jnp.int32, (128, 2 * REACH), 0)
    lane = lax.broadcasted_iota(jnp.int32, (128, 2 * REACH), 1)
    heads = ((feature < 64) == (lane < REACH)).astype(F32).astype(BF16)

    def products(z):
        grads = mixed_grad[z * 128 : (z + 1) * 128]
        both = [grads[:, i * REACH : (i + 1) * REACH] for i in range(2)]
        both = [jnp.concatenate([part, part], axis=1) * heads for part in both]
        own = mm_nt(both[0], po_ref[pairs[z], 0]) + mm_nt(both[1], po_ref[pairs[z], 1])
        return own, mm_nt(both[0], ph_ref[pairs[z], 0]), mm_nt(both[1], ph_ref[pairs[z], 1])

    def store(z, own, halo0, halo1):
        terms = jnp.concatenate([own, halo0, halo1], axis=1)
        out_ref[z * 128 : (z + 1) * 128] = terms.astype(BF16)
        return ()

    staged(list(range(4)), (products, store), BACK_GAP)


def backward_kernel(
    po_ref, ph_ref, wd, wo_ref, dec_ref, oz_ref, oc_ref, slope_ref, count_ref,
    send_ref, spread_ref, hidden_ref,
):
    own = dec_ref[...]
    spread = jnp.full((CH, ROWS), 0.5, F32)
    total = jnp.zeros((CH, ROWS), F32)
    for other in [oz_ref[i] for i in range(3)] + [oc_ref[i] for i in range(4)]:
        differ = own - other.astype(F32)
        square = differ * differ + 0.25
        inverse = lax.rsqrt(square)
        spread += square * inverse
        total += differ * inverse
    spread_ref[...] = spread
    node_grad = (slope_ref[...] - count_ref[:1] * total * (1.0 / (MEMBERS - 1))) * (1.0 / MEMBERS)
    high = node_grad.astype(BF16)
    rest = (node_grad - high.astype(F32)).astype(BF16)
    hidden_grad = (mm(wd[...], high) + mm(wd[...], rest)).astype(BF16)
    hidden_ref[...] = hidden_grad
    value_terms(1, hidden_grad, wo_ref, po_ref, ph_ref, send_ref)


def own_product_kernel(po_ref, ph_ref, wo_ref, hidden_ref, t_ref, out_ref, terms):
    value_terms(0, hidden_ref[...], wo_ref, po_ref, ph_ref, terms)
    out_ref[...] = mm_nt(t_ref[...], terms[...])


def product_kernel(own_ref, u_ref, recv_ref, out_ref):
    out_ref[...] = (own_ref[...] + mm_nt(u_ref[...], recv_ref[...])).astype(BF16)


def band_kernel(pieces_ref, out_ref):
    for i in range(8):
        rows = slice(i * 32, (i + 1) * 32)
        both = (pieces_ref[0, rows].astype(F32) + pieces_ref[1, rows].astype(F32)) + (
            pieces_ref[2, rows].astype(F32) + pieces_ref[3, rows].astype(F32)
        )
        for zh in range(4):
            out_ref[zh * 8 + i] = both[:, zh * 128 : (zh + 1) * 128].astype(BF16)


def stack_kernel(a_ref, b_ref, c_ref, d_ref, out_ref):
    for i, ref in enumerate((a_ref, b_ref, c_ref, d_ref)):
        out_ref[i] = ref[...]


def last_kernel(pieces_ref, out_ref):
    total = pieces_ref[0].astype(F32)
    for i in range(1, 32):
        total += pieces_ref[i].astype(F32)
    out_ref[...] = total


def crps_kernel(abs_ref, spread_ref, node_ref, out_ref):
    select = selector(node_ref)
    parts = thirds(spread_ref[...])
    spread = mm(parts[2], select) + mm(parts[1], select) + mm(parts[0], select)
    out_ref[...] = abs_ref[...] - spread * (1.0 / (2.0 * (MEMBERS - 1)))


AXES = ("zh", "core", "y", "zl", "x")
SIZES = (4, 2, 4, 2, 4)


def moved(value, move):
    pairs = []
    for i, (zh, core, y, zl, x) in enumerate(np.ndindex(*SIZES)):
        zh, band = move(core, zh, y * 8 + zl * 4 + x)
        if 0 <= band < BANDS:
            to = (zh % 4, core, band // 8, band // 4 % 2, band % 4)
            pairs.append((i, int(np.ravel_multi_index(to, SIZES))))
    return lax.ppermute(value, AXES, pairs)


def grouped(label):
    groups = {}
    for i, place in enumerate(np.ndindex(*SIZES)):
        groups.setdefault(label(*place), []).append(i)
    return list(groups.values())


FIRST = grouped(lambda zh, core, y, zl, x: (zh, core, zl, x if core else y))
SECOND = grouped(lambda zh, core, y, zl, x: (core, y if core else x))


def ring(chunks):
    return [chunks[0]] + [
        moved(chunks[k], lambda core, zh, band: (zh + (4 - k if core else k), band))
        for k in (2, 1, 3)
    ]


def body(inputs, norm_gain, w_query, w_key, w_value, w_out, w_decode, point_node, truth):
    states = inputs[0]
    gain = norm_gain[None]
    node = point_node[None]
    swap = [(0, 1), (1, 0)]
    half = ((REACH, D), BF16)
    wide = ((ROWS, D), BF16)
    matrix = ((D, D), BF16)
    row = ((2 * PAIRS, 2 * REACH), F32)
    first, second = call(
        split_kernel, [half, half], 0.2, [pltpu.SemaphoreType.DMA((2,))], hbm=1, keep=True
    )(states)
    first = moved(first, lambda core, zh, band: (zh, band - 1 if core else band + 1))
    second = moved(second, lambda core, zh, band: (zh, band + 1 if core else band - 1))
    (
        queries, normed, here, w_key, w_value, w_out, w_decode, gain, exp_own, mixed_own, top_own,
        sum_own,
    ) = call(
        project_kernel,
        [wide, wide, wide, matrix, matrix, matrix, ((D, CH), BF16), ((1, D), F32)]
        + [((PAIRS, 2, ROWS, 2 * REACH), BF16), ((PAIRS, 2, 128, REACH), F32), row, row],
        3.0,
        [
            pltpu.VMEM((D, D), BF16),
            pltpu.VMEM((ROWS, D), BF16),
            pltpu.VMEM((D, ROWS), BF16),
            pltpu.SemaphoreType.DMA((11,)),
        ],
        hbm=7,
        limit=20,
        keep=True,
    )(w_query, w_key, w_value, w_out, w_decode, gain, states)
    exp_halo, factors, decoded, decoded_half, normed_halo = call(
        attend_kernel,
        [((PAIRS, 2, REACH, 2 * REACH), BF16), ((PAIRS, 4, 2 * REACH), F32)]
        + [((CH, ROWS), F32), ((CH, ROWS), BF16), wide],
        3.0,
        [pltpu.VMEM((ROWS, D), BF16), pltpu.VMEM((D, ROWS), BF16), pltpu.VMEM((ROWS, D), BF16)],
        limit=20,
        keep=True,
    )(
        first, second, gain, w_key, w_value, queries, mixed_own, top_own, sum_own, here, w_out,
        w_decode,
    )
    along = ring([None, decoded_half, decoded_half, decoded_half])[1:]
    probs = [((PAIRS, 2, ROWS, 2 * REACH), BF16), ((PAIRS, 2, REACH, 2 * REACH), BF16)]
    turned = ((D, 2 * ROWS), BF16)
    abs_error, slope, count, turned, turned_send, own, probs_own, probs_halo = call(
        truth_kernel,
        [((CH, PTS), F32), ((CH, ROWS), F32), ((8, ROWS), F32), turned, turned]
        + [((CH, ROWS), BF16), *probs],
        2.0,
        keep=True,
    )(decoded, node, truth, normed, normed_halo, exp_own, exp_halo, factors)
    (along,) = call(stack_kernel, [((4, CH, ROWS), BF16)], 0.1)(*along, own)
    across = lax.ppermute(along, "core", swap)
    turned_other = lax.ppermute(turned_send, "core", swap)
    send, spread, hidden_grad = call(
        backward_kernel,
        [((512, 512), BF16), ((CH, ROWS), F32), ((D, ROWS), BF16)],
        2.0,
        keep=True,
    )(probs_own, probs_halo, w_decode, w_out, decoded, along, across, slope, count)
    received = lax.ppermute(send, "core", swap)
    (own_product,) = call(
        own_product_kernel, [((D, 512), F32)], 2.0, [pltpu.VMEM((512, 512), BF16)], keep=True
    )(probs_own, probs_halo, w_out, hidden_grad, turned)
    (product,) = call(product_kernel, [((D, 512), BF16)], 1.0)(own_product, turned_other, received)
    product = product.reshape(4, 256, 512)
    pieces = lax.all_to_all(product, AXES, 0, 0, axis_index_groups=FIRST)
    (blocks,) = call(band_kernel, [((32, 32, 128), BF16)], 0.1)(pieces)
    blocks = lax.all_to_all(blocks, AXES, 0, 0, axis_index_groups=SECOND)
    (crps_terms,) = call(crps_kernel, [((CH, PTS), F32)], 1.0)(abs_error, spread, node)
    (grad_value,) = call(last_kernel, [((32, 128), F32)], 0.1)(blocks)
    return crps_terms[None], grad_value


def solution(mesh):
    parts = Mesh(mesh.devices.reshape(4, 2, 4, 2, 4), ("zh", "core", "y", "zl", "x"))
    member = ("zh", "core")
    return jax.shard_map(
        body,
        mesh=parts,
        in_specs=(
            P(member, GRID, None), P(), P(), P(), P(), P(), P(), P(GRID), P(None, GRID),
        ),
        out_specs=(P(member, None, GRID), P(GRID, member)),
        check_vma=False,
    )
```

```python
import jax
import jax.numpy as jnp
import numpy as np
from jax import lax
from jax.experimental import pallas as pl
from jax.experimental.pallas import tpu as pltpu
from jax.sharding import Mesh, PartitionSpec as P

F32 = jnp.float32
BF16 = jnp.bfloat16
ROWS = 256
REACH = 128
D = 1024
PAIRS = 8
PTS = 1024
CH = 128
MEMBERS = 8
BANDS = 32
SPLIT = 8.0
OWN_GAP = 4
HALO_GAP = 4
BACK_GAP = 2
MASKED = -1e30
GRID = ("y", "zl", "x")

NT = (((1,), (1,)), ((), ()))


def mm(a, b):
    return jnp.dot(a, b, preferred_element_type=F32)


def mm_nt(a, b):
    return lax.dot_general(a, b, NT, preferred_element_type=F32)


def rms(states, gain):
    floats = states.astype(F32)
    meansq = jnp.mean(floats * floats, axis=-1, keepdims=True) + 1e-05
    return (floats * lax.rsqrt(meansq) * gain).astype(BF16)


def thirds(values):
    first = values.astype(BF16)
    rest = values - first.astype(F32)
    second = rest.astype(BF16)
    third = (rest - second.astype(F32)).astype(BF16)
    return first, second, third


def call(kernel, outs, cost, scratch=(), hbm=0, limit=16, keep=False, out_hbm=0):
    def run(*args):
        args = [
            pltpu.with_memory_space_constraint(arg, pltpu.HBM) if i < hbm else arg
            for i, arg in enumerate(args)
        ]
        in_specs = [pl.BlockSpec(memory_space=pltpu.HBM)] * hbm
        in_specs += [pl.BlockSpec(memory_space=pltpu.VMEM)] * (len(args) - hbm)
        other = pltpu.VMEM if keep else jax.ShapeDtypeStruct
        near = len(outs) - out_hbm
        shapes = [other(s, d) for s, d in outs[:near]] + [pltpu.HBM(s, d) for s, d in outs[near:]]
        out_specs = [pl.BlockSpec(memory_space=pltpu.VMEM)] * near
        out_specs += [pl.BlockSpec(memory_space=pltpu.HBM)] * out_hbm
        return pl.pallas_call(
            kernel,
            out_shape=shapes,
            in_specs=in_specs,
            out_specs=out_specs,
            scratch_shapes=list(scratch),
            compiler_params=pltpu.CompilerParams(vmem_limit_bytes=limit * 2**20),
            cost_estimate=pl.CostEstimate(
                flops=int(cost * 1e9), bytes_accessed=int(cost * 3e6), transcendentals=0
            ),
        )(*args)

    return run


def split_kernel(x_hbm, first_ref, second_ref, sems):
    core = lax.axis_index("core")
    copies = [
        pltpu.make_async_copy(
            x_hbm.at[pl.ds(pl.multiple_of(start * REACH, REACH), REACH)], ref, sems.at[i]
        )
        for i, (start, ref) in enumerate(((1 - core, first_ref), (core, second_ref)))
    ]
    for copy in copies:
        copy.start()
    for copy in copies:
        copy.wait()


def staged(items, stages, gap):
    kept = [(item,) for item in items]
    for step in range(len(items) + gap * (len(stages) - 1)):
        for s, stage in enumerate(stages):
            i = step - gap * s
            if 0 <= i < len(items):
                kept[i] = (items[i], *stage(*kept[i]))


BLOCKS = [(pair, block) for block in range(2) for pair in range(PAIRS)]


def head_parts():
    lane = lax.broadcasted_iota(jnp.int32, (REACH, 128), 1)
    low = (lane < 64).astype(F32).astype(BF16)
    high = (lane >= 64).astype(F32).astype(BF16)
    row_low = lax.broadcasted_iota(jnp.int32, (128, REACH), 0) < 64
    key = lax.broadcasted_iota(jnp.int32, (REACH, 2 * REACH), 0)
    query = lax.broadcasted_iota(jnp.int32, (REACH, 2 * REACH), 1) % REACH
    return low, high, row_low, key, query


def project_kernel(
    wq_ref, wk_ref, wv_ref, gain_ref, x_ref, q_ref, n_ref, e_ref, out_ref, top_ref, sum_ref, k, vt
):
    normed = rms(x_ref[...], gain_ref[...])
    n_ref[...] = normed
    q_ref[...] = mm(normed, wq_ref[...]).astype(BF16) * jnp.asarray(0.125, BF16)
    k[...] = mm(normed, wk_ref[...]).astype(BF16)
    vt[...] = mm(normed, wv_ref[...]).T.astype(BF16)
    low, high, row_low, key, query = head_parts()
    before = jnp.where(key <= query, 0.0, MASKED)
    after = jnp.where(key >= query, 0.0, MASKED)

    def scores(item):
        pair, block = item
        cols = slice(pair * 128, (pair + 1) * 128)
        both = q_ref[block * REACH : (block + 1) * REACH, cols]
        stacked = jnp.concatenate([both * low, both * high], axis=0)
        s0 = mm_nt(k[:REACH, cols], stacked)
        s1 = mm_nt(k[REACH:, cols], stacked)
        return (s0, s1 + before) if block == 0 else (s0 + after, s1)

    def softmax(item, s0, s1):
        pair, block = item
        n = pair * 2 + block
        top = jnp.max(jnp.maximum(s0, s1), axis=0, keepdims=True)
        e0 = jnp.exp(s0 - top)
        e1 = jnp.exp(s1 - top)
        top_ref[n : n + 1] = top
        sum_ref[n : n + 1] = jnp.sum(e0 + e1, axis=0, keepdims=True)
        e = jnp.concatenate([e0.astype(BF16), e1.astype(BF16)], axis=0)
        e_ref[pair, block] = e
        return (mm(vt[pair * 128 : (pair + 1) * 128, :], e),)

    def store(item, out):
        out_ref[item] = jnp.where(row_low, out[:, :REACH], out[:, REACH:])
        return ()

    staged(BLOCKS, (scores, softmax, store), OWN_GAP)


def attend_kernel(
    first_ref, second_ref, gain_ref, wk_ref, wv_ref, q_ref, out_ref, top_ref, sum_ref, x_ref, wo_ref, wd_ref,
    e_ref, factor_ref, dec_ref, dech_ref, nh_ref, kh, vht, mixed,
):
    band = band_index()
    gain = gain_ref[...]
    core = lax.axis_index("core")
    for start, ref in ((core, first_ref), (1 - core, second_ref)):
        nh_ref[pl.ds(pl.multiple_of(start * REACH, REACH), REACH)] = rms(ref[...], gain)
    halo = nh_ref[...]
    kh[...] = mm(halo, wk_ref[...]).astype(BF16)
    vht[...] = mm(halo, wv_ref[...]).T.astype(BF16)
    low, high, row_low, key, query = head_parts()
    first = jnp.where((key >= query) & (band > 0), 0.0, MASKED)
    last = jnp.where((key <= query) & (band < BANDS - 1), 0.0, MASKED)

    def scores(item):
        pair, block = item
        rows = slice(block * REACH, (block + 1) * REACH)
        cols = slice(pair * 128, (pair + 1) * 128)
        both = q_ref[rows, cols]
        stacked = jnp.concatenate([both * low, both * high], axis=0)
        return (mm_nt(kh[rows, cols], stacked) + (last if block else first),)

    def softmax(item, scores):
        pair, block = item
        n = pair * 2 + block
        top_own = top_ref[n : n + 1]
        top_halo = jnp.max(scores, axis=0, keepdims=True)
        e = jnp.exp(scores - top_halo)
        e_half = e.astype(BF16)
        e_ref[pair, block] = e_half
        top = jnp.maximum(top_own, top_halo)
        scale_own = jnp.exp(top_own - top)
        scale_halo = jnp.exp(top_halo - top)
        inv = 1.0 / (
            sum_ref[n : n + 1] * scale_own + jnp.sum(e, axis=0, keepdims=True) * scale_halo
        )
        scale_own *= inv
        scale_halo *= inv
        factor_ref[pair, 2 * block : 2 * block + 1] = scale_own
        factor_ref[pair, 2 * block + 1 : 2 * block + 2] = scale_halo
        cols = slice(pair * 128, (pair + 1) * 128)
        out = mm(vht[cols, block * REACH : (block + 1) * REACH], e_half)
        return out, scale_own, scale_halo

    def join(item, out, scale_own, scale_halo):
        pair, block = item
        out *= scale_halo
        out = jnp.where(row_low, out[:, :REACH], out[:, REACH:])
        own = jnp.where(row_low, scale_own[:, :REACH], scale_own[:, REACH:])
        out += out_ref[pair, block] * own
        cols = slice(pair * 128, (pair + 1) * 128)
        mixed[block * REACH : (block + 1) * REACH, cols] = out.T.astype(BF16)
        return ()

    staged(BLOCKS, (scores, softmax, join), HALO_GAP)
    projected = mm(mixed[...], wo_ref[...])
    hidden = (x_ref[...].astype(F32) + projected).astype(BF16)
    decoded = mm(hidden, wd_ref[...]).T
    dec_ref[...] = decoded
    dech_ref[...] = decoded.astype(BF16)


def band_index():
    return (lax.axis_index("y") * 2 + lax.axis_index("zl")) * 4 + lax.axis_index("x")


def selector(node_ref):
    node = lax.broadcasted_iota(jnp.int32, (ROWS, PTS), 0) + band_index() * ROWS
    return (node == node_ref[...]).astype(F32).astype(BF16)


def truth_kernel(
    dec_ref, node_ref, truth_ref, n_ref, nh_ref, eo_ref, eh_ref, factor_ref,
    abs_ref, slope_ref, count_ref, keep_ref, send_ref, own_ref, po_ref, ph_ref,
):
    own_ref[...] = dec_ref[...].astype(BF16)
    select = selector(node_ref)
    parts = thirds(dec_ref[...])
    pred = mm(parts[2], select) + mm(parts[1], select) + mm(parts[0], select)
    error = pred - truth_ref[...]
    square = error * error + 0.25
    inverse = lax.rsqrt(square)
    abs_ref[...] = square * inverse
    slope = error * inverse
    high = slope.astype(BF16)
    rest = (slope - high.astype(F32)).astype(BF16)
    slope_ref[...] = mm_nt(high, select) + mm_nt(rest, select)
    count_ref[...] = mm_nt(jnp.ones((16, PTS), BF16), select)[:8]
    core = lax.axis_index("core")
    for columns, ref in ((slice(0, ROWS), n_ref), (slice(ROWS, 2 * ROWS), nh_ref)):
        for g in range(BANDS):
            rows = ref[:, g * 32 : (g + 1) * 32].astype(F32).T.astype(BF16)
            by_x = g % 4 * 8 + g // 4
            for which, out_ref in ((core, keep_ref), (1 - core, send_ref)):
                start = pl.multiple_of(jnp.where(which == 0, by_x, g) * 32, 32)
                out_ref[pl.ds(start, 32), columns] = rows
    for pair in range(PAIRS):
        for block in range(2):
            factors = factor_ref[pair]
            own = eo_ref[pair, block].astype(F32) * factors[2 * block : 2 * block + 1]
            po_ref[pair, block] = own.astype(BF16)
            halo = eh_ref[pair, block].astype(F32) * factors[2 * block + 1 : 2 * block + 2]
            ph_ref[pair, block] = halo.astype(BF16)


def value_terms(which, hidden_grad, wo_ref, po_ref, ph_ref, out_ref):
    core = lax.axis_index("core")
    pairs = [2 * z + (core + which) % 2 for z in range(4)]
    rows = [wo_ref[pl.ds(pl.multiple_of(pair * 128, 128), 128), :] for pair in pairs]
    mixed_grad = mm(jnp.concatenate(rows, axis=0), hidden_grad).astype(BF16)
    feature = lax.broadcasted_iota(jnp.int32, (128, 2 * REACH), 0)
    lane = lax.broadcasted_iota(jnp.int32, (128, 2 * REACH), 1)
    heads = ((feature < 64) == (lane < REACH)).astype(F32).astype(BF16)

    def products(z):
        grads = mixed_grad[z * 128 : (z + 1) * 128]
        both = [grads[:, i * REACH : (i + 1) * REACH] for i in range(2)]
        both = [jnp.concatenate([part, part], axis=1) * heads for part in both]
        own = mm_nt(both[0], po_ref[pairs[z], 0]) + mm_nt(both[1], po_ref[pairs[z], 1])
        return own, mm_nt(both[0], ph_ref[pairs[z], 0]), mm_nt(both[1], ph_ref[pairs[z], 1])

    def store(z, own, halo0, halo1):
        terms = jnp.concatenate([own, halo0, halo1], axis=1)
        out_ref[z * 128 : (z + 1) * 128] = terms.astype(BF16)
        return ()

    staged(list(range(4)), (products, store), BACK_GAP)


def backward_kernel(
    po_ref, ph_ref, wd, wo_ref, dec_ref, oz_ref, oc_ref, slope_ref, count_ref,
    send_ref, spread_ref, hidden_ref,
):
    own = dec_ref[...]
    spread = jnp.full((CH, ROWS), 0.5, F32)
    total = jnp.zeros((CH, ROWS), F32)
    for other in [oz_ref[i] for i in range(3)] + [oc_ref[i] for i in range(4)]:
        differ = own - other.astype(F32)
        square = differ * differ + 0.25
        inverse = lax.rsqrt(square)
        spread += square * inverse
        total += differ * inverse
    spread_ref[...] = spread
    node_grad = (slope_ref[...] - count_ref[:1] * total * (1.0 / (MEMBERS - 1))) * (1.0 / MEMBERS)
    high = node_grad.astype(BF16)
    rest = (node_grad - high.astype(F32)).astype(BF16)
    hidden_grad = (mm(wd[...], high) + mm(wd[...], rest)).astype(BF16)
    hidden_ref[...] = hidden_grad
    value_terms(1, hidden_grad, wo_ref, po_ref, ph_ref, send_ref)


def own_product_kernel(
    po_ref, ph_ref, wo_ref, hidden_ref, t_ref, abs_ref, spread_ref, node_ref,
    out_ref, crps_hbm, terms, crps, sem,
):
    select = selector(node_ref)
    parts = thirds(spread_ref[...])
    spread = mm(parts[2], select) + mm(parts[1], select) + mm(parts[0], select)
    crps[...] = abs_ref[...] - spread * (1.0 / (2.0 * (MEMBERS - 1)))
    copy = pltpu.make_async_copy(crps, crps_hbm, sem)
    copy.start()
    value_terms(0, hidden_ref[...], wo_ref, po_ref, ph_ref, terms)
    out_ref[...] = mm_nt(t_ref[...], terms[...])
    copy.wait()


def product_kernel(own_ref, u_ref, recv_ref, out_ref):
    out_ref[...] = (own_ref[...] + mm_nt(u_ref[...], recv_ref[...])).astype(BF16)


def band_kernel(pieces_ref, out_ref):
    for i in range(8):
        rows = slice(i * 32, (i + 1) * 32)
        both = (pieces_ref[0, rows].astype(F32) + pieces_ref[1, rows].astype(F32)) + (
            pieces_ref[2, rows].astype(F32) + pieces_ref[3, rows].astype(F32)
        )
        for zh in range(4):
            out_ref[zh * 8 + i] = both[:, zh * 128 : (zh + 1) * 128].astype(BF16)


def stack_kernel(a_ref, b_ref, c_ref, d_ref, out_ref):
    for i, ref in enumerate((a_ref, b_ref, c_ref, d_ref)):
        out_ref[i] = ref[...]


def last_kernel(pieces_ref, out_ref):
    total = pieces_ref[0].astype(F32)
    for i in range(1, 32):
        total += pieces_ref[i].astype(F32)
    out_ref[...] = total


AXES = ("zh", "core", "y", "zl", "x")
SIZES = (4, 2, 4, 2, 4)


def moved(value, move):
    pairs = []
    for i, (zh, core, y, zl, x) in enumerate(np.ndindex(*SIZES)):
        zh, band = move(core, zh, y * 8 + zl * 4 + x)
        if 0 <= band < BANDS:
            to = (zh % 4, core, band // 8, band // 4 % 2, band % 4)
            pairs.append((i, int(np.ravel_multi_index(to, SIZES))))
    return lax.ppermute(value, AXES, pairs)


def grouped(label):
    groups = {}
    for i, place in enumerate(np.ndindex(*SIZES)):
        groups.setdefault(label(*place), []).append(i)
    return list(groups.values())


FIRST = grouped(lambda zh, core, y, zl, x: (zh, core, zl, x if core else y))
SECOND = grouped(lambda zh, core, y, zl, x: (core, y if core else x))


def ring(chunks):
    return [chunks[0]] + [
        moved(chunks[k], lambda core, zh, band: (zh + (4 - k if core else k), band))
        for k in (2, 1, 3)
    ]


def body(inputs, norm_gain, w_query, w_key, w_value, w_out, w_decode, point_node, truth):
    states = inputs[0]
    gain = norm_gain[None]
    node = point_node[None]
    swap = [(0, 1), (1, 0)]
    half = ((REACH, D), BF16)
    wide = ((ROWS, D), BF16)
    row = ((2 * PAIRS, 2 * REACH), F32)
    first, second = call(
        split_kernel, [half, half], SPLIT, [pltpu.SemaphoreType.DMA((2,))], hbm=1, keep=True
    )(states)
    first = moved(first, lambda core, zh, band: (zh, band - 1 if core else band + 1))
    second = moved(second, lambda core, zh, band: (zh, band + 1 if core else band - 1))
    queries, normed, exp_own, mixed_own, top_own, sum_own = call(
        project_kernel,
        [wide, wide, ((PAIRS, 2, ROWS, 2 * REACH), BF16), ((PAIRS, 2, 128, REACH), F32), row, row],
        3.0,
        [pltpu.VMEM((ROWS, D), BF16), pltpu.VMEM((D, ROWS), BF16)],
        limit=20,
        keep=True,
    )(w_query, w_key, w_value, gain, states)
    exp_halo, factors, decoded, decoded_half, normed_halo = call(
        attend_kernel,
        [((PAIRS, 2, REACH, 2 * REACH), BF16), ((PAIRS, 4, 2 * REACH), F32)]
        + [((CH, ROWS), F32), ((CH, ROWS), BF16), wide],
        3.0,
        [pltpu.VMEM((ROWS, D), BF16), pltpu.VMEM((D, ROWS), BF16), pltpu.VMEM((ROWS, D), BF16)],
        limit=20,
        keep=True,
    )(
        first, second, gain, w_key, w_value, queries, mixed_own, top_own, sum_own, states, w_out,
        w_decode,
    )
    along = ring([None, decoded_half, decoded_half, decoded_half])[1:]
    probs = [((PAIRS, 2, ROWS, 2 * REACH), BF16), ((PAIRS, 2, REACH, 2 * REACH), BF16)]
    turned = ((D, 2 * ROWS), BF16)
    abs_error, slope, count, turned, turned_send, own, probs_own, probs_halo = call(
        truth_kernel,
        [((CH, PTS), F32), ((CH, ROWS), F32), ((8, ROWS), F32), turned, turned]
        + [((CH, ROWS), BF16), *probs],
        2.0,
        keep=True,
    )(decoded, node, truth, normed, normed_halo, exp_own, exp_halo, factors)
    (along,) = call(stack_kernel, [((4, CH, ROWS), BF16)], 0.1)(*along, own)
    across = lax.ppermute(along, "core", swap)
    turned_other = lax.ppermute(turned_send, "core", swap)
    send, spread, hidden_grad = call(
        backward_kernel,
        [((512, 512), BF16), ((CH, ROWS), F32), ((D, ROWS), BF16)],
        2.0,
        keep=True,
    )(probs_own, probs_halo, w_decode, w_out, decoded, along, across, slope, count)
    received = lax.ppermute(send, "core", swap)
    own_product, crps_terms = call(
        own_product_kernel, [((D, 512), F32), ((CH, PTS), F32)], 2.0,
        [pltpu.VMEM((512, 512), BF16), pltpu.VMEM((CH, PTS), F32), pltpu.SemaphoreType.DMA],
        keep=True,
        out_hbm=1,
    )(probs_own, probs_halo, w_out, hidden_grad, turned, abs_error, spread, node)
    (product,) = call(product_kernel, [((D, 512), BF16)], 1.0)(own_product, turned_other, received)
    product = product.reshape(4, 256, 512)
    pieces = lax.all_to_all(product, AXES, 0, 0, axis_index_groups=FIRST)
    (blocks,) = call(band_kernel, [((32, 32, 128), BF16)], 0.1)(pieces)
    blocks = lax.all_to_all(blocks, AXES, 0, 0, axis_index_groups=SECOND)
    (grad_value,) = call(last_kernel, [((32, 128), F32)], 0.1)(blocks)
    return crps_terms[None], grad_value


def solution(mesh):
    parts = Mesh(mesh.devices.reshape(4, 2, 4, 2, 4), ("zh", "core", "y", "zl", "x"))
    member = ("zh", "core")
    return jax.shard_map(
        body,
        mesh=parts,
        in_specs=(
            P(member, GRID, None), P(), P(), P(), P(), P(), P(), P(GRID), P(None, GRID),
        ),
        out_specs=(P(member, None, GRID), P(GRID, member)),
        check_vma=False,
    )
```

```python
import jax
import jax.numpy as jnp
import numpy as np
from jax import lax
from jax.experimental import pallas as pl
from jax.experimental.pallas import tpu as pltpu
from jax.sharding import Mesh, PartitionSpec as P

F32 = jnp.float32
BF16 = jnp.bfloat16
ROWS = 256
REACH = 128
D = 1024
PAIRS = 8
PTS = 1024
CH = 128
MEMBERS = 8
BANDS = 32
SPLIT = 8.0
OWN_GAP = 4
HALO_GAP = 4
BACK_GAP = 2
MASKED = -1e30
GRID = ("y", "zl", "x")

NT = (((1,), (1,)), ((), ()))


def mm(a, b):
    return jnp.dot(a, b, preferred_element_type=F32)


def mm_nt(a, b):
    return lax.dot_general(a, b, NT, preferred_element_type=F32)


def rms(states, gain):
    floats = states.astype(F32)
    meansq = jnp.mean(floats * floats, axis=-1, keepdims=True) + 1e-05
    return (floats * lax.rsqrt(meansq) * gain).astype(BF16)


def thirds(values):
    first = values.astype(BF16)
    rest = values - first.astype(F32)
    second = rest.astype(BF16)
    third = (rest - second.astype(F32)).astype(BF16)
    return first, second, third


def call(kernel, outs, cost, scratch=(), hbm=0, limit=16, keep=False, out_hbm=0):
    def run(*args):
        args = [
            pltpu.with_memory_space_constraint(arg, pltpu.HBM) if i < hbm else arg
            for i, arg in enumerate(args)
        ]
        in_specs = [pl.BlockSpec(memory_space=pltpu.HBM)] * hbm
        in_specs += [pl.BlockSpec(memory_space=pltpu.VMEM)] * (len(args) - hbm)
        other = pltpu.VMEM if keep else jax.ShapeDtypeStruct
        near = len(outs) - out_hbm
        shapes = [other(s, d) for s, d in outs[:near]] + [pltpu.HBM(s, d) for s, d in outs[near:]]
        out_specs = [pl.BlockSpec(memory_space=pltpu.VMEM)] * near
        out_specs += [pl.BlockSpec(memory_space=pltpu.HBM)] * out_hbm
        return pl.pallas_call(
            kernel,
            out_shape=shapes,
            in_specs=in_specs,
            out_specs=out_specs,
            scratch_shapes=list(scratch),
            compiler_params=pltpu.CompilerParams(vmem_limit_bytes=limit * 2**20),
            cost_estimate=pl.CostEstimate(
                flops=int(cost * 1e9), bytes_accessed=int(cost * 3e6), transcendentals=0
            ),
        )(*args)

    return run


def split_kernel(x_hbm, first_ref, second_ref, sems):
    core = lax.axis_index("core")
    copies = [
        pltpu.make_async_copy(
            x_hbm.at[pl.ds(pl.multiple_of(start * REACH, REACH), REACH)], ref, sems.at[i]
        )
        for i, (start, ref) in enumerate(((1 - core, first_ref), (core, second_ref)))
    ]
    for copy in copies:
        copy.start()
    for copy in copies:
        copy.wait()


def staged(items, stages, gap):
    kept = [(item,) for item in items]
    for step in range(len(items) + gap * (len(stages) - 1)):
        for s, stage in enumerate(stages):
            i = step - gap * s
            if 0 <= i < len(items):
                kept[i] = (items[i], *stage(*kept[i]))


BLOCKS = [(pair, block) for block in range(2) for pair in range(PAIRS)]


def head_parts():
    lane = lax.broadcasted_iota(jnp.int32, (REACH, 128), 1)
    low = (lane < 64).astype(F32).astype(BF16)
    high = (lane >= 64).astype(F32).astype(BF16)
    row_low = lax.broadcasted_iota(jnp.int32, (128, REACH), 0) < 64
    key = lax.broadcasted_iota(jnp.int32, (REACH, 2 * REACH), 0)
    query = lax.broadcasted_iota(jnp.int32, (REACH, 2 * REACH), 1) % REACH
    return low, high, row_low, key, query


def project_kernel(
    wq_ref, wk_ref, wv_ref, gain_ref, x_ref, q_ref, n_ref, e_ref, out_ref, top_ref, sum_ref, k, vt
):
    normed = rms(x_ref[...], gain_ref[...])
    n_ref[...] = normed
    q_ref[...] = mm(normed, wq_ref[...]).astype(BF16) * jnp.asarray(0.125, BF16)
    k[...] = mm(normed, wk_ref[...]).astype(BF16)
    vt[...] = mm(normed, wv_ref[...]).T.astype(BF16)
    low, high, row_low, key, query = head_parts()
    before = jnp.where(key <= query, 0.0, MASKED)
    after = jnp.where(key >= query, 0.0, MASKED)

    def scores(item):
        pair, block = item
        cols = slice(pair * 128, (pair + 1) * 128)
        both = q_ref[block * REACH : (block + 1) * REACH, cols]
        stacked = jnp.concatenate([both * low, both * high], axis=0)
        s0 = mm_nt(k[:REACH, cols], stacked)
        s1 = mm_nt(k[REACH:, cols], stacked)
        return (s0, s1 + before) if block == 0 else (s0 + after, s1)

    def softmax(item, s0, s1):
        pair, block = item
        n = pair * 2 + block
        top = jnp.max(jnp.maximum(s0, s1), axis=0, keepdims=True)
        e0 = jnp.exp(s0 - top)
        e1 = jnp.exp(s1 - top)
        top_ref[n : n + 1] = top
        sum_ref[n : n + 1] = jnp.sum(e0 + e1, axis=0, keepdims=True)
        e = jnp.concatenate([e0.astype(BF16), e1.astype(BF16)], axis=0)
        e_ref[pair, block] = e
        return (mm(vt[pair * 128 : (pair + 1) * 128, :], e),)

    def store(item, out):
        out_ref[item] = jnp.where(row_low, out[:, :REACH], out[:, REACH:])
        return ()

    staged(BLOCKS, (scores, softmax, store), OWN_GAP)


def attend_kernel(
    first_ref, second_ref, gain_ref, wk_ref, wv_ref, q_ref, out_ref, top_ref, sum_ref, x_ref, wo_ref, wd_ref,
    e_ref, factor_ref, dec_ref, dech_ref, nh_ref, kh, vht, mixed,
):
    band = band_index()
    gain = gain_ref[...]
    core = lax.axis_index("core")
    for start, ref in ((core, first_ref), (1 - core, second_ref)):
        nh_ref[pl.ds(pl.multiple_of(start * REACH, REACH), REACH)] = rms(ref[...], gain)
    halo = nh_ref[...]
    kh[...] = mm(halo, wk_ref[...]).astype(BF16)
    vht[...] = mm(halo, wv_ref[...]).T.astype(BF16)
    low, high, row_low, key, query = head_parts()
    first = jnp.where((key >= query) & (band > 0), 0.0, MASKED)
    last = jnp.where((key <= query) & (band < BANDS - 1), 0.0, MASKED)

    def scores(item):
        pair, block = item
        rows = slice(block * REACH, (block + 1) * REACH)
        cols = slice(pair * 128, (pair + 1) * 128)
        both = q_ref[rows, cols]
        stacked = jnp.concatenate([both * low, both * high], axis=0)
        return (mm_nt(kh[rows, cols], stacked) + (last if block else first),)

    def softmax(item, scores):
        pair, block = item
        n = pair * 2 + block
        top_own = top_ref[n : n + 1]
        top_halo = jnp.max(scores, axis=0, keepdims=True)
        e = jnp.exp(scores - top_halo)
        e_half = e.astype(BF16)
        e_ref[pair, block] = e_half
        top = jnp.maximum(top_own, top_halo)
        scale_own = jnp.exp(top_own - top)
        scale_halo = jnp.exp(top_halo - top)
        inv = 1.0 / (
            sum_ref[n : n + 1] * scale_own + jnp.sum(e, axis=0, keepdims=True) * scale_halo
        )
        scale_own *= inv
        scale_halo *= inv
        factor_ref[pair, 2 * block : 2 * block + 1] = scale_own
        factor_ref[pair, 2 * block + 1 : 2 * block + 2] = scale_halo
        cols = slice(pair * 128, (pair + 1) * 128)
        out = mm(vht[cols, block * REACH : (block + 1) * REACH], e_half)
        return out, scale_own, scale_halo

    def join(item, out, scale_own, scale_halo):
        pair, block = item
        out *= scale_halo
        out = jnp.where(row_low, out[:, :REACH], out[:, REACH:])
        own = jnp.where(row_low, scale_own[:, :REACH], scale_own[:, REACH:])
        out += out_ref[pair, block] * own
        cols = slice(pair * 128, (pair + 1) * 128)
        mixed[block * REACH : (block + 1) * REACH, cols] = out.T.astype(BF16)
        return ()

    staged(BLOCKS, (scores, softmax, join), HALO_GAP)
    projected = mm(mixed[...], wo_ref[...])
    hidden = (x_ref[...].astype(F32) + projected).astype(BF16)
    decoded = mm(hidden, wd_ref[...]).T
    dec_ref[...] = decoded
    dech_ref[...] = decoded.astype(BF16)


def band_index():
    return (lax.axis_index("y") * 2 + lax.axis_index("zl")) * 4 + lax.axis_index("x")


def selector(node_ref):
    node = lax.broadcasted_iota(jnp.int32, (ROWS, PTS), 0) + band_index() * ROWS
    return (node == node_ref[...]).astype(F32).astype(BF16)


def truth_kernel(
    dec_ref, node_ref, truth_ref, n_ref, nh_ref, eo_ref, eh_ref, factor_ref,
    abs_ref, slope_ref, count_ref, keep_ref, send_ref, own_ref, po_ref, ph_ref,
):
    own_ref[...] = dec_ref[...].astype(BF16)
    select = selector(node_ref)
    parts = thirds(dec_ref[...])
    pred = mm(parts[2], select) + mm(parts[1], select) + mm(parts[0], select)
    error = pred - truth_ref[...]
    square = error * error + 0.25
    inverse = lax.rsqrt(square)
    abs_ref[...] = square * inverse
    slope = error * inverse
    high = slope.astype(BF16)
    rest = (slope - high.astype(F32)).astype(BF16)
    slope_ref[...] = mm_nt(high, select) + mm_nt(rest, select)
    count_ref[...] = mm_nt(jnp.ones((16, PTS), BF16), select)[:8]
    core = lax.axis_index("core")
    for columns, ref in ((slice(0, ROWS), n_ref), (slice(ROWS, 2 * ROWS), nh_ref)):
        for k in range(8):
            block = ref[:, k * 128 : (k + 1) * 128].astype(F32).T.astype(BF16)
            for g in range(k * 4, k * 4 + 4):
                rows = block[g % 4 * 32 : (g % 4 + 1) * 32]
                by_x = g % 4 * 8 + g // 4
                for which, out_ref in ((core, keep_ref), (1 - core, send_ref)):
                    start = pl.multiple_of(jnp.where(which == 0, by_x, g) * 32, 32)
                    out_ref[pl.ds(start, 32), columns] = rows
    for pair in range(PAIRS):
        for block in range(2):
            factors = factor_ref[pair]
            own = eo_ref[pair, block].astype(F32) * factors[2 * block : 2 * block + 1]
            po_ref[pair, block] = own.astype(BF16)
            halo = eh_ref[pair, block].astype(F32) * factors[2 * block + 1 : 2 * block + 2]
            ph_ref[pair, block] = halo.astype(BF16)


def value_terms(which, hidden_grad, wo_ref, po_ref, ph_ref, out_ref):
    core = lax.axis_index("core")
    pairs = [2 * z + (core + which) % 2 for z in range(4)]
    rows = [wo_ref[pl.ds(pl.multiple_of(pair * 128, 128), 128), :] for pair in pairs]
    mixed_grad = mm(jnp.concatenate(rows, axis=0), hidden_grad).astype(BF16)
    feature = lax.broadcasted_iota(jnp.int32, (128, 2 * REACH), 0)
    lane = lax.broadcasted_iota(jnp.int32, (128, 2 * REACH), 1)
    heads = ((feature < 64) == (lane < REACH)).astype(F32).astype(BF16)

    def products(z):
        grads = mixed_grad[z * 128 : (z + 1) * 128]
        both = [grads[:, i * REACH : (i + 1) * REACH] for i in range(2)]
        both = [jnp.concatenate([part, part], axis=1) * heads for part in both]
        own = mm_nt(both[0], po_ref[pairs[z], 0]) + mm_nt(both[1], po_ref[pairs[z], 1])
        return own, mm_nt(both[0], ph_ref[pairs[z], 0]), mm_nt(both[1], ph_ref[pairs[z], 1])

    def store(z, own, halo0, halo1):
        terms = jnp.concatenate([own, halo0, halo1], axis=1)
        out_ref[z * 128 : (z + 1) * 128] = terms.astype(BF16)
        return ()

    staged(list(range(4)), (products, store), BACK_GAP)


def backward_kernel(
    po_ref, ph_ref, wd, wo_ref, dec_ref, oz_ref, oc_ref, slope_ref, count_ref,
    send_ref, spread_ref, hidden_ref,
):
    own = dec_ref[...]
    spread = jnp.full((CH, ROWS), 0.5, F32)
    total = jnp.zeros((CH, ROWS), F32)
    for other in [oz_ref[i] for i in range(3)] + [oc_ref[i] for i in range(4)]:
        differ = own - other.astype(F32)
        square = differ * differ + 0.25
        inverse = lax.rsqrt(square)
        spread += square * inverse
        total += differ * inverse
    spread_ref[...] = spread
    node_grad = (slope_ref[...] - count_ref[:1] * total * (1.0 / (MEMBERS - 1))) * (1.0 / MEMBERS)
    high = node_grad.astype(BF16)
    rest = (node_grad - high.astype(F32)).astype(BF16)
    hidden_grad = (mm(wd[...], high) + mm(wd[...], rest)).astype(BF16)
    hidden_ref[...] = hidden_grad
    value_terms(1, hidden_grad, wo_ref, po_ref, ph_ref, send_ref)


def own_product_kernel(
    po_ref, ph_ref, wo_ref, hidden_ref, t_ref, abs_ref, spread_ref, node_ref,
    out_ref, crps_hbm, terms, crps, sem,
):
    select = selector(node_ref)
    parts = thirds(spread_ref[...])
    spread = mm(parts[2], select) + mm(parts[1], select) + mm(parts[0], select)
    crps[...] = abs_ref[...] - spread * (1.0 / (2.0 * (MEMBERS - 1)))
    copy = pltpu.make_async_copy(crps, crps_hbm, sem)
    copy.start()
    value_terms(0, hidden_ref[...], wo_ref, po_ref, ph_ref, terms)
    out_ref[...] = mm_nt(t_ref[...], terms[...])
    copy.wait()


def product_kernel(own_ref, u_ref, recv_ref, out_ref):
    out_ref[...] = (own_ref[...] + mm_nt(u_ref[...], recv_ref[...])).astype(BF16)


def band_kernel(pieces_ref, out_ref):
    for i in range(8):
        rows = slice(i * 32, (i + 1) * 32)
        both = (pieces_ref[0, rows].astype(F32) + pieces_ref[1, rows].astype(F32)) + (
            pieces_ref[2, rows].astype(F32) + pieces_ref[3, rows].astype(F32)
        )
        for zh in range(4):
            out_ref[zh * 8 + i] = both[:, zh * 128 : (zh + 1) * 128].astype(BF16)


def stack_kernel(a_ref, b_ref, c_ref, d_ref, out_ref):
    for i, ref in enumerate((a_ref, b_ref, c_ref, d_ref)):
        out_ref[i] = ref[...]


def last_kernel(pieces_ref, out_ref):
    total = pieces_ref[0].astype(F32)
    for i in range(1, 32):
        total += pieces_ref[i].astype(F32)
    out_ref[...] = total


AXES = ("zh", "core", "y", "zl", "x")
SIZES = (4, 2, 4, 2, 4)


def moved(value, move):
    pairs = []
    for i, (zh, core, y, zl, x) in enumerate(np.ndindex(*SIZES)):
        zh, band = move(core, zh, y * 8 + zl * 4 + x)
        if 0 <= band < BANDS:
            to = (zh % 4, core, band // 8, band // 4 % 2, band % 4)
            pairs.append((i, int(np.ravel_multi_index(to, SIZES))))
    return lax.ppermute(value, AXES, pairs)


def grouped(label):
    groups = {}
    for i, place in enumerate(np.ndindex(*SIZES)):
        groups.setdefault(label(*place), []).append(i)
    return list(groups.values())


FIRST = grouped(lambda zh, core, y, zl, x: (zh, core, zl, x if core else y))
SECOND = grouped(lambda zh, core, y, zl, x: (core, y if core else x))


def ring(chunks):
    return [chunks[0]] + [
        moved(chunks[k], lambda core, zh, band: (zh + (4 - k if core else k), band))
        for k in (2, 1, 3)
    ]


def body(inputs, norm_gain, w_query, w_key, w_value, w_out, w_decode, point_node, truth):
    states = inputs[0]
    gain = norm_gain[None]
    node = point_node[None]
    swap = [(0, 1), (1, 0)]
    half = ((REACH, D), BF16)
    wide = ((ROWS, D), BF16)
    row = ((2 * PAIRS, 2 * REACH), F32)
    first, second = call(
        split_kernel, [half, half], SPLIT, [pltpu.SemaphoreType.DMA((2,))], hbm=1, keep=True
    )(states)
    first = moved(first, lambda core, zh, band: (zh, band - 1 if core else band + 1))
    second = moved(second, lambda core, zh, band: (zh, band + 1 if core else band - 1))
    queries, normed, exp_own, mixed_own, top_own, sum_own = call(
        project_kernel,
        [wide, wide, ((PAIRS, 2, ROWS, 2 * REACH), BF16), ((PAIRS, 2, 128, REACH), F32), row, row],
        3.0,
        [pltpu.VMEM((ROWS, D), BF16), pltpu.VMEM((D, ROWS), BF16)],
        limit=20,
        keep=True,
    )(w_query, w_key, w_value, gain, states)
    exp_halo, factors, decoded, decoded_half, normed_halo = call(
        attend_kernel,
        [((PAIRS, 2, REACH, 2 * REACH), BF16), ((PAIRS, 4, 2 * REACH), F32)]
        + [((CH, ROWS), F32), ((CH, ROWS), BF16), wide],
        3.0,
        [pltpu.VMEM((ROWS, D), BF16), pltpu.VMEM((D, ROWS), BF16), pltpu.VMEM((ROWS, D), BF16)],
        limit=20,
        keep=True,
    )(
        first, second, gain, w_key, w_value, queries, mixed_own, top_own, sum_own, states, w_out,
        w_decode,
    )
    along = ring([None, decoded_half, decoded_half, decoded_half])[1:]
    probs = [((PAIRS, 2, ROWS, 2 * REACH), BF16), ((PAIRS, 2, REACH, 2 * REACH), BF16)]
    turned = ((D, 2 * ROWS), BF16)
    abs_error, slope, count, turned, turned_send, own, probs_own, probs_halo = call(
        truth_kernel,
        [((CH, PTS), F32), ((CH, ROWS), F32), ((8, ROWS), F32), turned, turned]
        + [((CH, ROWS), BF16), *probs],
        2.0,
        keep=True,
    )(decoded, node, truth, normed, normed_halo, exp_own, exp_halo, factors)
    (along,) = call(stack_kernel, [((4, CH, ROWS), BF16)], 0.1)(*along, own)
    across = lax.ppermute(along, "core", swap)
    turned_other = lax.ppermute(turned_send, "core", swap)
    send, spread, hidden_grad = call(
        backward_kernel,
        [((512, 512), BF16), ((CH, ROWS), F32), ((D, ROWS), BF16)],
        2.0,
        keep=True,
    )(probs_own, probs_halo, w_decode, w_out, decoded, along, across, slope, count)
    received = lax.ppermute(send, "core", swap)
    own_product, crps_terms = call(
        own_product_kernel, [((D, 512), F32), ((CH, PTS), F32)], 2.0,
        [pltpu.VMEM((512, 512), BF16), pltpu.VMEM((CH, PTS), F32), pltpu.SemaphoreType.DMA],
        keep=True,
        out_hbm=1,
    )(probs_own, probs_halo, w_out, hidden_grad, turned, abs_error, spread, node)
    (product,) = call(product_kernel, [((D, 512), BF16)], 1.0)(own_product, turned_other, received)
    product = product.reshape(4, 256, 512)
    pieces = lax.all_to_all(product, AXES, 0, 0, axis_index_groups=FIRST)
    (blocks,) = call(band_kernel, [((32, 32, 128), BF16)], 0.1)(pieces)
    blocks = lax.all_to_all(blocks, AXES, 0, 0, axis_index_groups=SECOND)
    (grad_value,) = call(last_kernel, [((32, 128), F32)], 0.1)(blocks)
    return crps_terms[None], grad_value


def solution(mesh):
    parts = Mesh(mesh.devices.reshape(4, 2, 4, 2, 4), ("zh", "core", "y", "zl", "x"))
    member = ("zh", "core")
    return jax.shard_map(
        body,
        mesh=parts,
        in_specs=(
            P(member, GRID, None), P(), P(), P(), P(), P(), P(), P(GRID), P(None, GRID),
        ),
        out_specs=(P(member, None, GRID), P(GRID, member)),
        check_vma=False,
    )
```

```python
import jax
import jax.numpy as jnp
import numpy as np
from jax import lax
from jax.experimental import pallas as pl
from jax.experimental.pallas import tpu as pltpu
from jax.sharding import Mesh, PartitionSpec as P

F32 = jnp.float32
BF16 = jnp.bfloat16
ROWS = 256
REACH = 128
D = 1024
PAIRS = 8
PTS = 1024
CH = 128
MEMBERS = 8
BANDS = 32
SPLIT = 8.0
OWN_GAP = 4
HALO_GAP = 4
BACK_GAP = 2
MASKED = -1e30
GRID = ("y", "zl", "x")

NT = (((1,), (1,)), ((), ()))


def mm(a, b):
    return jnp.dot(a, b, preferred_element_type=F32)


def mm_nt(a, b):
    return lax.dot_general(a, b, NT, preferred_element_type=F32)


def rms(states, gain):
    floats = states.astype(F32)
    meansq = jnp.mean(floats * floats, axis=-1, keepdims=True) + 1e-05
    return (floats * lax.rsqrt(meansq) * gain).astype(BF16)


def thirds(values):
    first = values.astype(BF16)
    rest = values - first.astype(F32)
    second = rest.astype(BF16)
    third = (rest - second.astype(F32)).astype(BF16)
    return first, second, third


def call(kernel, outs, cost, scratch=(), hbm=0, limit=16, keep=False, out_hbm=0):
    def run(*args):
        args = [
            pltpu.with_memory_space_constraint(arg, pltpu.HBM) if i < hbm else arg
            for i, arg in enumerate(args)
        ]
        in_specs = [pl.BlockSpec(memory_space=pltpu.HBM)] * hbm
        in_specs += [pl.BlockSpec(memory_space=pltpu.VMEM)] * (len(args) - hbm)
        other = pltpu.VMEM if keep else jax.ShapeDtypeStruct
        near = len(outs) - out_hbm
        shapes = [other(s, d) for s, d in outs[:near]] + [pltpu.HBM(s, d) for s, d in outs[near:]]
        out_specs = [pl.BlockSpec(memory_space=pltpu.VMEM)] * near
        out_specs += [pl.BlockSpec(memory_space=pltpu.HBM)] * out_hbm
        return pl.pallas_call(
            kernel,
            out_shape=shapes,
            in_specs=in_specs,
            out_specs=out_specs,
            scratch_shapes=list(scratch),
            compiler_params=pltpu.CompilerParams(vmem_limit_bytes=limit * 2**20),
            cost_estimate=pl.CostEstimate(
                flops=int(cost * 1e9), bytes_accessed=int(cost * 3e6), transcendentals=0
            ),
        )(*args)

    return run


def split_kernel(x_hbm, first_ref, second_ref, sems):
    core = lax.axis_index("core")
    copies = [
        pltpu.make_async_copy(
            x_hbm.at[pl.ds(pl.multiple_of(start * REACH, REACH), REACH)], ref, sems.at[i]
        )
        for i, (start, ref) in enumerate(((1 - core, first_ref), (core, second_ref)))
    ]
    for copy in copies:
        copy.start()
    for copy in copies:
        copy.wait()


def staged(items, stages, gap):
    kept = [(item,) for item in items]
    for step in range(len(items) + gap * (len(stages) - 1)):
        for s, stage in enumerate(stages):
            i = step - gap * s
            if 0 <= i < len(items):
                kept[i] = (items[i], *stage(*kept[i]))


BLOCKS = [(pair, block) for block in range(2) for pair in range(PAIRS)]


def head_parts():
    lane = lax.broadcasted_iota(jnp.int32, (REACH, 128), 1)
    low = (lane < 64).astype(F32).astype(BF16)
    high = (lane >= 64).astype(F32).astype(BF16)
    row_low = lax.broadcasted_iota(jnp.int32, (128, REACH), 0) < 64
    key = lax.broadcasted_iota(jnp.int32, (REACH, 2 * REACH), 0)
    query = lax.broadcasted_iota(jnp.int32, (REACH, 2 * REACH), 1) % REACH
    return low, high, row_low, key, query


def project_kernel(
    wq_ref, wk_ref, wv_ref, gain_ref, x_ref, q_ref, n_ref, e_ref, out_ref, top_ref, sum_ref, k, vt
):
    normed = rms(x_ref[...], gain_ref[...])
    n_ref[...] = normed
    q_ref[...] = mm(normed, wq_ref[...]).astype(BF16) * jnp.asarray(0.125, BF16)
    k[...] = mm(normed, wk_ref[...]).astype(BF16)
    vt[...] = mm(normed, wv_ref[...]).T.astype(BF16)
    low, high, row_low, key, query = head_parts()
    before = jnp.where(key <= query, 0.0, MASKED)
    after = jnp.where(key >= query, 0.0, MASKED)

    def scores(item):
        pair, block = item
        cols = slice(pair * 128, (pair + 1) * 128)
        both = q_ref[block * REACH : (block + 1) * REACH, cols]
        stacked = jnp.concatenate([both * low, both * high], axis=0)
        s0 = mm_nt(k[:REACH, cols], stacked)
        s1 = mm_nt(k[REACH:, cols], stacked)
        return (s0, s1 + before) if block == 0 else (s0 + after, s1)

    def softmax(item, s0, s1):
        pair, block = item
        n = pair * 2 + block
        top = jnp.max(jnp.maximum(s0, s1), axis=0, keepdims=True)
        e0 = jnp.exp(s0 - top)
        e1 = jnp.exp(s1 - top)
        top_ref[n : n + 1] = top
        sum_ref[n : n + 1] = jnp.sum(e0 + e1, axis=0, keepdims=True)
        e = jnp.concatenate([e0.astype(BF16), e1.astype(BF16)], axis=0)
        e_ref[pair, block] = e
        return (mm(vt[pair * 128 : (pair + 1) * 128, :], e),)

    def store(item, out):
        out_ref[item] = jnp.where(row_low, out[:, :REACH], out[:, REACH:])
        return ()

    staged(BLOCKS, (scores, softmax, store), OWN_GAP)


def attend_kernel(
    first_ref, second_ref, gain_ref, wk_ref, wv_ref, q_ref, out_ref, top_ref, sum_ref, x_ref, wo_ref, wd_ref,
    e_ref, factor_ref, dec_ref, dech_ref, nh_ref, kh, vht, mixed,
):
    band = band_index()
    gain = gain_ref[...]
    core = lax.axis_index("core")
    for start, ref in ((core, first_ref), (1 - core, second_ref)):
        nh_ref[pl.ds(pl.multiple_of(start * REACH, REACH), REACH)] = rms(ref[...], gain)
    halo = nh_ref[...]
    kh[...] = mm(halo, wk_ref[...]).astype(BF16)
    vht[...] = mm(halo, wv_ref[...]).T.astype(BF16)
    low, high, row_low, key, query = head_parts()
    first = jnp.where((key >= query) & (band > 0), 0.0, MASKED)
    last = jnp.where((key <= query) & (band < BANDS - 1), 0.0, MASKED)

    def scores(item):
        pair, block = item
        rows = slice(block * REACH, (block + 1) * REACH)
        cols = slice(pair * 128, (pair + 1) * 128)
        both = q_ref[rows, cols]
        stacked = jnp.concatenate([both * low, both * high], axis=0)
        return (mm_nt(kh[rows, cols], stacked) + (last if block else first),)

    def softmax(item, scores):
        pair, block = item
        n = pair * 2 + block
        top_own = top_ref[n : n + 1]
        top_halo = jnp.max(scores, axis=0, keepdims=True)
        e = jnp.exp(scores - top_halo)
        e_half = e.astype(BF16)
        e_ref[pair, block] = e_half
        top = jnp.maximum(top_own, top_halo)
        scale_own = jnp.exp(top_own - top)
        scale_halo = jnp.exp(top_halo - top)
        inv = 1.0 / (
            sum_ref[n : n + 1] * scale_own + jnp.sum(e, axis=0, keepdims=True) * scale_halo
        )
        scale_own *= inv
        scale_halo *= inv
        factor_ref[pair, 2 * block : 2 * block + 1] = scale_own
        factor_ref[pair, 2 * block + 1 : 2 * block + 2] = scale_halo
        cols = slice(pair * 128, (pair + 1) * 128)
        out = mm(vht[cols, block * REACH : (block + 1) * REACH], e_half)
        return out, scale_own, scale_halo

    def join(item, out, scale_own, scale_halo):
        pair, block = item
        out *= scale_halo
        out = jnp.where(row_low, out[:, :REACH], out[:, REACH:])
        own = jnp.where(row_low, scale_own[:, :REACH], scale_own[:, REACH:])
        out += out_ref[pair, block] * own
        cols = slice(pair * 128, (pair + 1) * 128)
        mixed[block * REACH : (block + 1) * REACH, cols] = out.T.astype(BF16)
        return ()

    staged(BLOCKS, (scores, softmax, join), HALO_GAP)
    projected = mm(mixed[...], wo_ref[...])
    hidden = (x_ref[...].astype(F32) + projected).astype(BF16)
    decoded = mm(hidden, wd_ref[...]).T
    dec_ref[...] = decoded
    dech_ref[...] = decoded.astype(BF16)


def band_index():
    return (lax.axis_index("y") * 2 + lax.axis_index("zl")) * 4 + lax.axis_index("x")


def selector(node_ref):
    node = lax.broadcasted_iota(jnp.int32, (ROWS, PTS), 0) + band_index() * ROWS
    return (node == node_ref[...]).astype(F32).astype(BF16)


def truth_kernel(
    dec_ref, node_ref, truth_ref, n_ref, nh_ref, eo_ref, eh_ref, factor_ref,
    abs_ref, slope_ref, count_ref, keep_ref, send_ref, own_ref, po_ref, ph_ref,
):
    own_ref[...] = dec_ref[...].astype(BF16)
    select = selector(node_ref)
    parts = thirds(dec_ref[...])
    pred = mm(parts[2], select) + mm(parts[1], select) + mm(parts[0], select)
    error = pred - truth_ref[...]
    square = error * error + 0.25
    inverse = lax.rsqrt(square)
    abs_ref[...] = square * inverse
    slope = error * inverse
    high = slope.astype(BF16)
    rest = (slope - high.astype(F32)).astype(BF16)
    slope_ref[...] = mm_nt(high, select) + mm_nt(rest, select)
    count_ref[...] = mm_nt(jnp.ones((16, PTS), BF16), select)[:8]
    core = lax.axis_index("core")
    for columns, ref in ((slice(0, ROWS), n_ref), (slice(ROWS, 2 * ROWS), nh_ref)):
        for g in range(BANDS):
            rows = ref[:, g * 32 : (g + 1) * 32].astype(F32).T.astype(BF16)
            by_x = g % 4 * 8 + g // 4
            for which, out_ref in ((core, keep_ref), (1 - core, send_ref)):
                start = pl.multiple_of(jnp.where(which == 0, by_x, g) * 32, 32)
                out_ref[pl.ds(start, 32), columns] = rows
    for pair in range(PAIRS):
        for block in range(2):
            factors = factor_ref[pair]
            own = eo_ref[pair, block].astype(F32) * factors[2 * block : 2 * block + 1]
            po_ref[pair, block] = own.astype(BF16)
            halo = eh_ref[pair, block].astype(F32) * factors[2 * block + 1 : 2 * block + 2]
            ph_ref[pair, block] = halo.astype(BF16)


def value_terms(which, hidden_grad, wo_ref, po_ref, ph_ref, out_ref):
    core = lax.axis_index("core")
    pairs = [2 * z + (core + which) % 2 for z in range(4)]
    rows = [wo_ref[pl.ds(pl.multiple_of(pair * 128, 128), 128), :] for pair in pairs]
    mixed_grad = mm(jnp.concatenate(rows, axis=0), hidden_grad).astype(BF16)
    feature = lax.broadcasted_iota(jnp.int32, (128, 2 * REACH), 0)
    lane = lax.broadcasted_iota(jnp.int32, (128, 2 * REACH), 1)
    heads = ((feature < 64) == (lane < REACH)).astype(F32).astype(BF16)

    def products(z):
        grads = mixed_grad[z * 128 : (z + 1) * 128]
        both = [grads[:, i * REACH : (i + 1) * REACH] for i in range(2)]
        both = [jnp.concatenate([part, part], axis=1) * heads for part in both]
        own = mm_nt(both[0], po_ref[pairs[z], 0]) + mm_nt(both[1], po_ref[pairs[z], 1])
        return own, mm_nt(both[0], ph_ref[pairs[z], 0]), mm_nt(both[1], ph_ref[pairs[z], 1])

    def store(z, own, halo0, halo1):
        terms = jnp.concatenate([own, halo0, halo1], axis=1)
        out_ref[z * 128 : (z + 1) * 128] = terms.astype(BF16)
        return ()

    staged(list(range(4)), (products, store), BACK_GAP)


def backward_kernel(
    po_ref, ph_ref, wd, wo_ref, dec_ref, oz_ref, oc_ref, slope_ref, count_ref,
    send_ref, spread_ref, hidden_ref,
):
    own = dec_ref[...]
    spread = jnp.full((CH, ROWS), 0.5, F32)
    total = jnp.zeros((CH, ROWS), F32)
    for other in [oz_ref[i] for i in range(3)] + [oc_ref[i] for i in range(4)]:
        differ = own - other.astype(F32)
        square = differ * differ + 0.25
        inverse = lax.rsqrt(square)
        spread += square * inverse
        total += differ * inverse
    spread_ref[...] = spread
    node_grad = (slope_ref[...] - count_ref[:1] * total * (1.0 / (MEMBERS - 1))) * (1.0 / MEMBERS)
    hidden_grad = mm(wd[...], node_grad.astype(BF16)).astype(BF16)
    hidden_ref[...] = hidden_grad
    value_terms(1, hidden_grad, wo_ref, po_ref, ph_ref, send_ref)


def own_product_kernel(
    po_ref, ph_ref, wo_ref, hidden_ref, t_ref, abs_ref, spread_ref, node_ref,
    out_ref, crps_hbm, terms, crps, sem,
):
    select = selector(node_ref)
    parts = thirds(spread_ref[...])
    spread = mm(parts[2], select) + mm(parts[1], select) + mm(parts[0], select)
    crps[...] = abs_ref[...] - spread * (1.0 / (2.0 * (MEMBERS - 1)))
    copy = pltpu.make_async_copy(crps, crps_hbm, sem)
    copy.start()
    value_terms(0, hidden_ref[...], wo_ref, po_ref, ph_ref, terms)
    out_ref[...] = mm_nt(t_ref[...], terms[...])
    copy.wait()


def product_kernel(own_ref, u_ref, recv_ref, out_ref):
    out_ref[...] = (own_ref[...] + mm_nt(u_ref[...], recv_ref[...])).astype(BF16)


def band_kernel(pieces_ref, out_ref):
    for i in range(8):
        rows = slice(i * 32, (i + 1) * 32)
        both = (pieces_ref[0, rows].astype(F32) + pieces_ref[1, rows].astype(F32)) + (
            pieces_ref[2, rows].astype(F32) + pieces_ref[3, rows].astype(F32)
        )
        for zh in range(4):
            out_ref[zh * 8 + i] = both[:, zh * 128 : (zh + 1) * 128].astype(BF16)


def stack_kernel(a_ref, b_ref, c_ref, d_ref, out_ref):
    for i, ref in enumerate((a_ref, b_ref, c_ref, d_ref)):
        out_ref[i] = ref[...]


def last_kernel(pieces_ref, out_ref):
    total = pieces_ref[0].astype(F32)
    for i in range(1, 32):
        total += pieces_ref[i].astype(F32)
    out_ref[...] = total


AXES = ("zh", "core", "y", "zl", "x")
SIZES = (4, 2, 4, 2, 4)


def moved(value, move):
    pairs = []
    for i, (zh, core, y, zl, x) in enumerate(np.ndindex(*SIZES)):
        zh, band = move(core, zh, y * 8 + zl * 4 + x)
        if 0 <= band < BANDS:
            to = (zh % 4, core, band // 8, band // 4 % 2, band % 4)
            pairs.append((i, int(np.ravel_multi_index(to, SIZES))))
    return lax.ppermute(value, AXES, pairs)


def grouped(label):
    groups = {}
    for i, place in enumerate(np.ndindex(*SIZES)):
        groups.setdefault(label(*place), []).append(i)
    return list(groups.values())


FIRST = grouped(lambda zh, core, y, zl, x: (zh, core, zl, x if core else y))
SECOND = grouped(lambda zh, core, y, zl, x: (core, y if core else x))


def ring(chunks):
    return [chunks[0]] + [
        moved(chunks[k], lambda core, zh, band: (zh + (4 - k if core else k), band))
        for k in (2, 1, 3)
    ]


def body(inputs, norm_gain, w_query, w_key, w_value, w_out, w_decode, point_node, truth):
    states = inputs[0]
    gain = norm_gain[None]
    node = point_node[None]
    swap = [(0, 1), (1, 0)]
    half = ((REACH, D), BF16)
    wide = ((ROWS, D), BF16)
    row = ((2 * PAIRS, 2 * REACH), F32)
    first, second = call(
        split_kernel, [half, half], SPLIT, [pltpu.SemaphoreType.DMA((2,))], hbm=1, keep=True
    )(states)
    first = moved(first, lambda core, zh, band: (zh, band - 1 if core else band + 1))
    second = moved(second, lambda core, zh, band: (zh, band + 1 if core else band - 1))
    queries, normed, exp_own, mixed_own, top_own, sum_own = call(
        project_kernel,
        [wide, wide, ((PAIRS, 2, ROWS, 2 * REACH), BF16), ((PAIRS, 2, 128, REACH), F32), row, row],
        3.0,
        [pltpu.VMEM((ROWS, D), BF16), pltpu.VMEM((D, ROWS), BF16)],
        limit=20,
        keep=True,
    )(w_query, w_key, w_value, gain, states)
    exp_halo, factors, decoded, decoded_half, normed_halo = call(
        attend_kernel,
        [((PAIRS, 2, REACH, 2 * REACH), BF16), ((PAIRS, 4, 2 * REACH), F32)]
        + [((CH, ROWS), F32), ((CH, ROWS), BF16), wide],
        3.0,
        [pltpu.VMEM((ROWS, D), BF16), pltpu.VMEM((D, ROWS), BF16), pltpu.VMEM((ROWS, D), BF16)],
        limit=20,
        keep=True,
    )(
        first, second, gain, w_key, w_value, queries, mixed_own, top_own, sum_own, states, w_out,
        w_decode,
    )
    along = ring([None, decoded_half, decoded_half, decoded_half])[1:]
    probs = [((PAIRS, 2, ROWS, 2 * REACH), BF16), ((PAIRS, 2, REACH, 2 * REACH), BF16)]
    turned = ((D, 2 * ROWS), BF16)
    abs_error, slope, count, turned, turned_send, own, probs_own, probs_halo = call(
        truth_kernel,
        [((CH, PTS), F32), ((CH, ROWS), F32), ((8, ROWS), F32), turned, turned]
        + [((CH, ROWS), BF16), *probs],
        2.0,
        keep=True,
    )(decoded, node, truth, normed, normed_halo, exp_own, exp_halo, factors)
    (along,) = call(stack_kernel, [((4, CH, ROWS), BF16)], 0.1)(*along, own)
    across = lax.ppermute(along, "core", swap)
    turned_other = lax.ppermute(turned_send, "core", swap)
    send, spread, hidden_grad = call(
        backward_kernel,
        [((512, 512), BF16), ((CH, ROWS), F32), ((D, ROWS), BF16)],
        2.0,
        keep=True,
    )(probs_own, probs_halo, w_decode, w_out, decoded, along, across, slope, count)
    received = lax.ppermute(send, "core", swap)
    own_product, crps_terms = call(
        own_product_kernel, [((D, 512), F32), ((CH, PTS), F32)], 2.0,
        [pltpu.VMEM((512, 512), BF16), pltpu.VMEM((CH, PTS), F32), pltpu.SemaphoreType.DMA],
        keep=True,
        out_hbm=1,
    )(probs_own, probs_halo, w_out, hidden_grad, turned, abs_error, spread, node)
    (product,) = call(product_kernel, [((D, 512), BF16)], 1.0)(own_product, turned_other, received)
    product = product.reshape(4, 256, 512)
    pieces = lax.all_to_all(product, AXES, 0, 0, axis_index_groups=FIRST)
    (blocks,) = call(band_kernel, [((32, 32, 128), BF16)], 0.1)(pieces)
    blocks = lax.all_to_all(blocks, AXES, 0, 0, axis_index_groups=SECOND)
    (grad_value,) = call(last_kernel, [((32, 128), F32)], 0.1)(blocks)
    return crps_terms[None], grad_value


def solution(mesh):
    parts = Mesh(mesh.devices.reshape(4, 2, 4, 2, 4), ("zh", "core", "y", "zl", "x"))
    member = ("zh", "core")
    return jax.shard_map(
        body,
        mesh=parts,
        in_specs=(
            P(member, GRID, None), P(), P(), P(), P(), P(), P(), P(GRID), P(None, GRID),
        ),
        out_specs=(P(member, None, GRID), P(GRID, member)),
        check_vma=False,
    )
```
